128 devices in a mesh: seq: 8 (over x, y_hi), head: 16 (over z, y_lo, core).
Axes of the slice: x: 4, y: 4 (y_hi: 2, y_lo: 2; y = y_hi * 2 + y_lo), z: 4, core: 2. Of those that a mesh axis runs over, the one named last changes fastest.
Arguments:
- token_ids: int32 [131072], P(('seq', 'head')), may hold values from 0 to 511
- bar_mask: int32 [131072], P(('seq', 'head')), may hold values from 0 to 1, as said below
- embed: bfloat16 [512, 1024], replicated, may hold values from -6 to 6
- mask_embed: bfloat16 [1024], replicated, may hold values from -6 to 6
- local_gain: bfloat16 [1024], replicated, may hold values from 0.25 to 1.75
- local_query: bfloat16 [1024, 1024], replicated, may hold values from -100 to 100
- local_key: bfloat16 [1024, 1024], replicated, may hold values from -1 to 1
- local_value: bfloat16 [1024, 1024], replicated, may hold values from -0.1875 to 0.1875
- local_out: bfloat16 [1024, 1024], replicated, may hold values from -0.1875 to 0.1875
- coarse_gain: bfloat16 [1024], replicated, may hold values from 0.25 to 1.75
- coarse_query: bfloat16 [1024, 1024], replicated, may hold values from -100 to 100
- coarse_key: bfloat16 [1024, 1024], replicated, may hold values from -1 to 1
- coarse_value: bfloat16 [1024, 1024], replicated, may hold values from -0.1875 to 0.1875
- coarse_out: bfloat16 [1024, 1024], replicated, may hold values from -0.1875 to 0.1875
Outputs:
- block_out: bfloat16 [131072, 1024], P(('seq', 'head'))
The draws below stay inside these ranges and needn't reach their ends.
Inputs may be any that keep to these rules, and one draw needn't show every extreme that they name: bar_mask is constant on each bar, a run of 1 to 96 consecutive tokens.
All inputs are finite; a program needn't handle non-finite values.
Results may differ from the reference program's by a relative error of at most 0.024.
Values may be sent and summed in bfloat16 or wider, within the bound.
No kernel may reach another device: no remote copies, remote signals or barrier semaphores. Data moves between devices by JAX's collectives and lax.ppermute only.
A program may use at most 192 MiB of HBM per device.

```python
import math
import jax
import jax.numpy as jnp
import numpy as np
from jax import lax

D = 1024
HEADS = 16
HEAD_DIM = 64
VOCAB = 512
HALF_WIN = 512
POOL = 64
TOK_DEV = 1024
TOKENS = 131072
POOLED = 2048


def shared_matrix(key, salt):
    sub = jax.random.fold_in(key, salt)
    base = jnp.clip(jax.random.normal(sub, (D, D), jnp.float32), -4.0, 4.0)
    return base * D ** (-0.5)


def query_matrix(key, salt):
    noise = shared_matrix(key, salt + 1)
    return noise.astype(jnp.bfloat16)


def draw_local_key(key, part):
    return shared_matrix(key, 101).astype(jnp.bfloat16)


def draw_local_query(key, part):
    return query_matrix(key, 101)


def draw_coarse_key(key, part):
    return shared_matrix(key, 202).astype(jnp.bfloat16)


def draw_coarse_query(key, part):
    return query_matrix(key, 202)


def pair_table(key):
    own = jax.random.normal(jax.random.fold_in(key, 2), (VOCAB, D), jnp.float32)
    rows = own
    return jnp.clip(rows, -6.0, 6.0).astype(jnp.bfloat16)


def draw_embed(key, part):
    key = jax.random.fold_in(key, 7)
    return pair_table(key)


def draw_bar_mask(key, part):
    key = jax.random.fold_in(key, 41)
    place = jnp.arange(TOKENS, dtype=jnp.int32)
    starts = (jax.random.randint(jax.random.fold_in(key, 1), (TOKENS,), 0, 48) == 0) | (place % 96 == 0)
    bar_index = jnp.cumsum(starts.astype(jnp.int32)) - 1
    flags = jax.random.randint(jax.random.fold_in(key, 2), (TOKENS,), 0, 4) == 0
    chosen = jax.random.randint(jax.random.fold_in(key, 3), (), 0, TOKENS)
    other = (chosen + TOKENS // 2) % TOKENS
    masked = (flags[bar_index] | (bar_index == bar_index[chosen])) & (bar_index != bar_index[other])
    return masked.astype(jnp.int32)


def place_ends(array, own_key, smallest, top_value):
    dims = array.shape
    spot = [jax.random.randint(jax.random.fold_in(own_key, axis), (), 0, dims[axis]) for axis in range(len(dims))]
    array = array.at[tuple(spot)].set(smallest)
    longest = dims.index(max(dims))
    spot[longest] = (spot[longest] + 1) % dims[longest]
    return array.at[tuple(spot)].set(top_value)


def cumulative_ranks(number_of, skew):
    portions = [(1 << 20) // math.isqrt(standing ** skew) + 1 for standing in range(1, number_of + 1)]
    deviation = 1 + sum(portions) // (1 << 30)
    return np.cumsum(np.array([max(1, weight // deviation) for weight in portions]))


def ranked(stream_key, extent, count, slope):
    table = cumulative_ranks(count, slope)
    lot = jax.random.randint(jax.random.fold_in(stream_key, 1), extent, 0, int(table[count - 1]))
    grade = jnp.searchsorted(jnp.asarray(table, jnp.int32), lot, side="right")
    return jax.random.permutation(jax.random.fold_in(stream_key, 2), count)[grade].astype(jnp.int32)


def gaussian(stream_key, dims, deviation, bound, kind=jnp.bfloat16):
    result = jax.random.normal(stream_key, dims, jnp.float32) * deviation
    return jnp.minimum(jnp.maximum(result, -bound), bound).astype(kind)


def setup_inputs(seed: int = 0) -> dict:
    streams_of = jax.random.split(jax.random.key(seed), 15)
    token_ids = place_ends(ranked(streams_of[0], (TOKENS,), VOCAB, 2), jax.random.fold_in(streams_of[0], 3), 0, VOCAB - 1).astype(jnp.int32)
    bar_mask = draw_bar_mask(jax.random.fold_in(streams_of[14], 71), 0)
    embed = draw_embed(jax.random.fold_in(streams_of[14], 71), 0)
    mask_embed = gaussian(streams_of[3], (D,), 1.0, 6.0)
    local_gain = jnp.clip(1.0 + 0.15 * jax.random.normal(streams_of[4], (D,), jnp.float32), 0.25, 1.75).astype(jnp.bfloat16)
    local_query = draw_local_query(jax.random.fold_in(streams_of[14], 71), 0)
    local_key = draw_local_key(jax.random.fold_in(streams_of[14], 71), 0)
    local_value = gaussian(streams_of[7], (D, D), D ** -0.5, 0.1875)
    local_out = gaussian(streams_of[8], (D, D), D ** -0.5, 0.1875)
    coarse_gain = jnp.clip(1.0 + 0.15 * jax.random.normal(streams_of[9], (D,), jnp.float32), 0.25, 1.75).astype(jnp.bfloat16)
    coarse_query = draw_coarse_query(jax.random.fold_in(streams_of[14], 71), 0)
    coarse_key = draw_coarse_key(jax.random.fold_in(streams_of[14], 71), 0)
    coarse_value = gaussian(streams_of[12], (D, D), D ** -0.5, 0.1875)
    coarse_out = gaussian(streams_of[13], (D, D), D ** -0.5, 0.1875)
    return dict(token_ids=token_ids, bar_mask=bar_mask, embed=embed, mask_embed=mask_embed, local_gain=local_gain, local_query=local_query, local_key=local_key, local_value=local_value, local_out=local_out, coarse_gain=coarse_gain, coarse_query=coarse_query, coarse_key=coarse_key, coarse_value=coarse_value, coarse_out=coarse_out)


def normalize(rows, gain):
    wide = rows.astype(jnp.float32)
    scaled = wide * lax.rsqrt(lax.optimization_barrier(jnp.mean(wide * wide, axis=-1, keepdims=True)) + 1e-05)
    return (scaled * gain.astype(jnp.float32)).astype(jnp.bfloat16)

def local_block(q_rows, k_rows, v_rows, q_start, k_start, total, reach):
    count = q_rows.shape[0]
    span = k_rows.shape[0]
    width = q_rows.shape[1] // HEADS
    qh = q_rows.astype(jnp.float32).reshape(count, HEADS, width)
    kh = k_rows.astype(jnp.float32).reshape(span, HEADS, width)
    vh = v_rows.astype(jnp.float32).reshape(span, HEADS, width)
    scores = jnp.einsum('qhd,khd->hqk', qh, kh) * width ** (-0.5)
    q_pos = q_start + jnp.arange(count, dtype=jnp.int32)
    k_pos = k_start + jnp.arange(span, dtype=jnp.int32)
    valid = (jnp.abs(q_pos[:, None] - k_pos[None, :]) <= reach) & (k_pos[None, :] >= 0) & (k_pos[None, :] < total)
    scores = jnp.where(valid[None], scores, -1e+30)
    top = lax.optimization_barrier(jnp.max(scores, axis=-1, keepdims=True))
    probs = jnp.exp(scores - top)
    probs = (probs / lax.optimization_barrier(jnp.sum(probs, axis=-1, keepdims=True))).astype(jnp.bfloat16)
    mixed = jnp.einsum('hqk,khd->qhd', probs.astype(jnp.float32), vh)
    return mixed.reshape(count, HEADS * width).astype(jnp.bfloat16)

def reference(token_ids, bar_mask, embed, mask_embed, local_gain, local_query, local_key, local_value, local_out, coarse_gain, coarse_query, coarse_key, coarse_value, coarse_out):
    inputs = jnp.where(bar_mask[:, None] == 1, mask_embed[None, :], embed[token_ids])
    normed = normalize(inputs, local_gain)
    queries = jnp.dot(normed, local_query, preferred_element_type=jnp.float32).astype(jnp.bfloat16)
    keys = jnp.dot(normed, local_key, preferred_element_type=jnp.float32).astype(jnp.bfloat16)
    values = jnp.dot(normed, local_value, preferred_element_type=jnp.float32).astype(jnp.bfloat16)
    block = min(512, TOK_DEV)
    padded_k = jnp.pad(keys, ((HALF_WIN, HALF_WIN), (0, 0)))
    padded_v = jnp.pad(values, ((HALF_WIN, HALF_WIN), (0, 0)))

    def one_block(index):
        first = index * block
        q_rows = lax.dynamic_slice_in_dim(queries, first, block, 0)
        k_rows = lax.dynamic_slice_in_dim(padded_k, first, block + 2 * HALF_WIN, 0)
        v_rows = lax.dynamic_slice_in_dim(padded_v, first, block + 2 * HALF_WIN, 0)
        return local_block(q_rows, k_rows, v_rows, first, first - HALF_WIN, TOKENS, HALF_WIN)
    local_att = lax.map(one_block, jnp.arange(TOKENS // block, dtype=jnp.int32)).reshape(TOKENS, D)
    mid = (inputs.astype(jnp.float32) + jnp.dot(local_att, local_out, preferred_element_type=jnp.float32)).astype(jnp.bfloat16)
    pooled = lax.optimization_barrier(jnp.mean(mid.astype(jnp.float32).reshape(POOLED, POOL, D), axis=1)).astype(jnp.bfloat16)
    coarse_normed = normalize(pooled, coarse_gain)
    cq = jnp.dot(coarse_normed, coarse_query, preferred_element_type=jnp.float32).astype(jnp.bfloat16)
    ck = jnp.dot(coarse_normed, coarse_key, preferred_element_type=jnp.float32).astype(jnp.bfloat16)
    cv = jnp.dot(coarse_normed, coarse_value, preferred_element_type=jnp.float32).astype(jnp.bfloat16)
    cqh = cq.astype(jnp.float32).reshape(POOLED, HEADS, HEAD_DIM).transpose(1, 0, 2)
    ckh = ck.astype(jnp.float32).reshape(POOLED, HEADS, HEAD_DIM).transpose(1, 0, 2)
    cvh = cv.astype(jnp.float32).reshape(POOLED, HEADS, HEAD_DIM).transpose(1, 0, 2)

    def one_head(triple):
        hq, hk, hv = triple
        scores = jnp.dot(hq, hk.T, precision=lax.Precision.HIGHEST) * HEAD_DIM ** (-0.5)
        top = lax.optimization_barrier(jnp.max(scores, axis=-1, keepdims=True))
        probs = jnp.exp(scores - top)
        probs = probs / lax.optimization_barrier(jnp.sum(probs, axis=-1, keepdims=True))
        return jnp.dot(probs, hv, precision=lax.Precision.HIGHEST)
    coarse_att = lax.map(one_head, (cqh, ckh, cvh)).transpose(1, 0, 2).reshape(POOLED, D).astype(jnp.bfloat16)
    lifted = jnp.dot(coarse_att, coarse_out, preferred_element_type=jnp.float32)
    return (mid.astype(jnp.float32) + jnp.repeat(lifted, POOL, axis=0)).astype(jnp.bfloat16)
```

```python
import functools
import math

import jax
import jax.numpy as jnp
from jax import lax
from jax.experimental import pallas as pl
from jax.experimental.pallas import tpu as pltpu
from jax.sharding import Mesh
from jax.sharding import PartitionSpec as P

D = 1024
HEADS = 16
WIDTH = 64
VOCAB = 512
ROWS = VOCAB + 16
HALF_WIN = 512
POOL = 64
TILE = 512
SUB = 256
GROUP = 4
COLS = GROUP * WIDTH
VROWS = WIDTH + 16
MIB = 1 << 20
ALL = ("x_hi", "x_lo", "y_hi", "z_hi", "z_lo", "y_lo", "core")
RING = ("z_hi", "z_lo", "core")
PLANE = ("x_hi", "x_lo", "y_hi", "y_lo")
F32 = jnp.float32
BF16 = jnp.bfloat16


def dot(a, b):
    return jnp.dot(a, b, preferred_element_type=F32)


def dot_nt(a, b):
    return lax.dot_general(a, b, (((1,), (1,)), ((), ())), preferred_element_type=F32)


def dot_tn(a, b):
    return lax.dot_general(a, b, (((0,), (0,)), ((), ())), preferred_element_type=F32)


def normalize(rows, gain):
    wide = rows.astype(F32)
    scaled = wide * lax.rsqrt(jnp.mean(wide * wide, axis=-1, keepdims=True) + 1e-05)
    return (scaled * gain.astype(F32)).astype(BF16)


def rounded(x):
    return x.astype(BF16).astype(F32)


def one_hot(ids):
    event = lax.broadcasted_iota(jnp.int32, (ROWS, ids.shape[1]), 0) + 1
    return jnp.where(event == ids, 1.0, 0.0).astype(BF16)


def local_kernel(
    low, own, high, mask_embed, gain, cgain, embed_hbm, lq, lk, lv, wout_hbm, cq, ck, cv,
    att, payload,
    hot, logs, scores, pooled_in, matt, embed, local_w, weights, normed, k3, vt, att_out,
    sem_e, sem_l, sem_w, sem_o,
):
    step = pl.program_id(0)
    rows = att.shape[0]
    steps = HEADS // GROUP
    embed_copy = pltpu.make_async_copy(embed_hbm, embed, sem_e)

    def local_copy(i, g):
        src = (lq, lk, lv)[i].at[:, pl.ds(pl.multiple_of(g * COLS, COLS), COLS)]
        return pltpu.make_async_copy(src, local_w.at[i, g], sem_l.at[i, g])

    late_copies = [
        pltpu.make_async_copy(src, weights.at[i], sem_w.at[i])
        for i, src in enumerate((wout_hbm, cq, ck, cv))
    ]

    def out_copy(g):
        dst = att.at[:, pl.ds(pl.multiple_of(g * COLS, COLS), COLS)]
        return pltpu.make_async_copy(att_out.at[g], dst, sem_o.at[g])

    @pl.when(step == 0)
    def _():
        embed_copy.start()
        for g in range(steps):
            for i in range(3):
                local_copy(i, g).start()
        for copy in late_copies:
            copy.start()
        hot[:, 0:HALF_WIN] = one_hot(low[...].reshape(1, HALF_WIN))
        hot[:, HALF_WIN : HALF_WIN + rows] = one_hot(own[...].reshape(1, rows))
        hot[:, HALF_WIN + rows :] = one_hot(high[...].reshape(1, HALF_WIN))
        j = lax.broadcasted_iota(jnp.int32, (SUB, SUB), 0)
        i = lax.broadcasted_iota(jnp.int32, (SUB, SUB), 1)
        first = jnp.where(j >= i, 1.0, 0.0).astype(BF16)
        last = jnp.where(j <= i, 1.0, 0.0).astype(BF16)
        every = jnp.ones((SUB, SUB), BF16)
        span = 2 * HALF_WIN // SUB
        for t in range(rows // SUB):
            block = lambda b: hot[:, (t + b) * SUB : (t + b + 1) * SUB]
            inner = block(1)
            for b in range(2, span):
                inner = inner + block(b)
            count = dot(block(0), first) + dot(inner, every) + dot(block(span), last)
            logs[:, t * SUB : (t + 1) * SUB] = jnp.where(
                count > 0.0, jnp.log(jnp.maximum(count, 1.0)) * math.log2(math.e), -1e30
            )
        row = lax.broadcasted_iota(jnp.int32, (16, rows), 0)
        col = lax.broadcasted_iota(jnp.int32, (16, rows), 1)
        member = jnp.where(col // POOL == row, 1.0 / POOL, 0.0).astype(BF16)
        share = dot_nt(member, hot[:, HALF_WIN : HALF_WIN + rows])
        embed_copy.wait()
        mask_row = mask_embed[...].reshape(1, D)
        gain_row = gain[...].reshape(1, D)
        pooled_in[...] = dot(share[:, 0:VOCAB].astype(BF16), embed[...]) + share[
            :, VOCAB : VOCAB + 1
        ] * mask_row.astype(F32)
        normed[0:VOCAB, :] = normalize(embed[...], gain_row)
        keep = lax.broadcasted_iota(jnp.int32, (16, D), 0) == 0
        row = jnp.broadcast_to(normalize(mask_row, gain_row).astype(F32), (16, D))
        normed[VOCAB:ROWS, :] = jnp.where(keep, row, 0.0).astype(BF16)

    for i in range(3):
        local_copy(i, step).wait()
    q = rounded(dot(normed[...], local_w[0, step]))
    qt = q[0:VOCAB].T.astype(BF16)
    qm = jnp.broadcast_to(q[VOCAB : VOCAB + 1], (128, COLS)).T
    k = rounded(dot(normed[...], local_w[1, step])) * (math.log2(math.e) * WIDTH**-0.5)
    k_a = k.astype(BF16)
    rest = k - k_a.astype(F32)
    k_b = rest.astype(BF16)
    k_c = (rest - k_b.astype(F32)).astype(BF16)
    v = rounded(dot(normed[...], local_w[2, step]))
    v_t = v[0:VOCAB].T
    v_m = jnp.broadcast_to(v[VOCAB : VOCAB + 1], (128, COLS)).T
    ones = jnp.where(lax.broadcasted_iota(jnp.int32, (16, VOCAB), 0) == 0, 1.0, 0.0)
    vm = []
    for h in range(GROUP):
        s = slice(h * WIDTH, (h + 1) * WIDTH)
        k3[h] = jnp.concatenate([k_a[:, s], k_b[:, s], k_c[:, s]], axis=1)
        vt[h] = jnp.concatenate([v_t[s], ones], axis=0).astype(BF16)
        vm.append(jnp.concatenate([v_m[s], ones[:, 0:128]], axis=0))

    queries = []
    for t in range(rows // TILE):
        own_cols = slice(HALF_WIN + t * TILE, HALF_WIN + (t + 1) * TILE)
        masked = hot[VOCAB:ROWS, own_cols].astype(F32)[0:1]
        x = dot(qt, hot[0:VOCAB, own_cols])
        x = x + jnp.concatenate([qm] * (TILE // 128), axis=1) * masked
        queries.append(x.astype(BF16))

    units = [(t, h) for t in range(rows // TILE) for h in range(GROUP)]

    def score(u):
        t, h = units[u]
        q_h = queries[t][h * WIDTH : (h + 1) * WIDTH]
        s = dot(k3[h], jnp.concatenate([q_h, q_h, q_h], axis=0))
        s = s + logs[:, t * TILE : (t + 1) * TILE]
        scores[u % 2] = s
        return jnp.max(s, axis=0, keepdims=True)

    def mix(u, top):
        h = units[u][1]
        probs = jnp.exp2((scores[u % 2] - top).astype(BF16))
        mixed = dot(vt[h], probs[0:VOCAB])
        last = probs[VOCAB:ROWS].astype(F32)[0:1]
        mixed = mixed + jnp.concatenate([vm[h]] * (TILE // 128), axis=1) * last
        return mixed[0:WIDTH] * (1.0 / mixed[WIDTH : WIDTH + 1])

    top = score(0)
    held = None
    for u, (t, h) in enumerate(units):
        later = score(u + 1) if u + 1 < len(units) else None
        mixed = mix(u, top)
        top = later
        if h % 2 == 0:
            held = mixed
            continue
        out = jnp.concatenate([held, mixed], axis=0).T
        cols = slice((h - 1) * WIDTH, (h + 1) * WIDTH)
        att_out[step, t * TILE : (t + 1) * TILE, cols] = out.astype(BF16)
        each = TILE // POOL
        mean = jnp.sum(out.reshape(each, POOL, 128), axis=1) * (1.0 / POOL)
        matt[step, t * each : (t + 1) * each, cols] = mean
    out_copy(step).start()

    @pl.when(step == steps - 1)
    def _():
        for copy in late_copies:
            copy.wait()
        mean = jnp.concatenate([matt[g] for g in range(steps)], axis=1)
        head = mean.astype(BF16)
        tail = (mean - head.astype(F32)).astype(BF16)
        lifted = dot(jnp.concatenate([head, tail], axis=0), weights[0])
        pooled = (pooled_in[...] + lifted[0:16] + lifted[16:32]).astype(BF16)
        coarse = normalize(pooled, cgain[...].reshape(1, D))
        q = rounded(dot(coarse, weights[1]))
        k = rounded(dot(coarse, weights[2]))
        v = rounded(dot(coarse, weights[3]))
        for h in range(HEADS):
            s = slice(h * WIDTH, (h + 1) * WIDTH)
            kv = jnp.concatenate([k[:, s], v[:, s]], axis=1)
            qq = jnp.concatenate([q[0:8, s], q[8:16, s]], axis=1)
            payload[h] = jnp.concatenate([kv, qq], axis=0).astype(BF16)
        for g in range(steps):
            out_copy(g).wait()


def local_attention(low, own, high, mask_embed, gain, cgain, *arrays):
    steps = HEADS // GROUP
    rows = own.shape[0]
    whole = lambda shape: pl.BlockSpec(shape, lambda g: (0,) * len(shape))
    hbm = pl.BlockSpec(memory_space=pl.ANY)
    small = (low, own, high, mask_embed, gain, cgain)
    return pl.pallas_call(
        local_kernel,
        grid=(steps,),
        in_specs=[whole(x.shape) for x in small] + [hbm] * len(arrays),
        out_specs=[hbm, whole((HEADS, 24, 128))],
        out_shape=[
            jax.ShapeDtypeStruct((rows, D), BF16),
            jax.ShapeDtypeStruct((HEADS, 24, 128), BF16),
        ],
        scratch_shapes=[
            pltpu.VMEM((ROWS, rows + 2 * HALF_WIN), BF16),
            pltpu.VMEM((ROWS, rows), F32),
            pltpu.VMEM((2, ROWS, TILE), F32),
            pltpu.VMEM((16, D), F32),
            pltpu.VMEM((steps, rows // POOL, COLS), F32),
            pltpu.VMEM((VOCAB, D), BF16),
            pltpu.VMEM((3, steps, D, COLS), BF16),
            pltpu.VMEM((4, D, D), BF16),
            pltpu.VMEM((ROWS, D), BF16),
            pltpu.VMEM((GROUP, ROWS, 3 * WIDTH), BF16),
            pltpu.VMEM((GROUP, VROWS, VOCAB), BF16),
            pltpu.VMEM((steps, rows, COLS), BF16),
            pltpu.SemaphoreType.DMA(()),
            pltpu.SemaphoreType.DMA((3, steps)),
            pltpu.SemaphoreType.DMA((4,)),
            pltpu.SemaphoreType.DMA((steps,)),
        ],
        compiler_params=pltpu.CompilerParams(vmem_limit_bytes=60 * MIB),
        cost_estimate=pl.CostEstimate(
            flops=16 * rows * ROWS * D, bytes_accessed=20 * MIB, transcendentals=rows * ROWS * HEADS
        ),
        name="local",
    )(*small, *arrays)


def mid_kernel(ids, att, embed, mask_embed, wout, mid):
    hot = one_hot(ids[...].reshape(1, SUB))
    total = dot(att[...], wout[...]) + dot_tn(hot[0:VOCAB], embed[...])
    row = jnp.broadcast_to(mask_embed[...].reshape(1, D), (16, D))
    total = total + dot_tn(hot[VOCAB:ROWS], row)
    mid[...] = total.astype(BF16)


def make_mid(ids, att, embed, mask_embed, wout):
    rows = att.shape[0]
    whole = lambda shape: pl.BlockSpec(shape, lambda g: (0,) * len(shape))
    return pl.pallas_call(
        mid_kernel,
        grid=(rows // SUB,),
        in_specs=[
            pl.BlockSpec((SUB,), lambda g: (g,)),
            pl.BlockSpec((SUB, D), lambda g: (g, 0)),
            whole((VOCAB, D)),
            whole((D,)),
            whole((D, D)),
        ],
        out_specs=pl.BlockSpec((SUB, D), lambda g: (g, 0)),
        out_shape=jax.ShapeDtypeStruct((rows, D), BF16),
        compiler_params=pltpu.CompilerParams(vmem_limit_bytes=60 * MIB),
        cost_estimate=pl.CostEstimate(
            flops=2 * rows * (ROWS + D) * D, bytes_accessed=8 * MIB, transcendentals=0
        ),
        name="mid",
    )(ids, att, embed, mask_embed, wout)


def coarse_kernel(q, kv, out):
    x = q[...].astype(F32).reshape(q.shape[0] * 8, 128) * WIDTH**-0.5
    low = lax.broadcasted_iota(jnp.int32, x.shape, 1) < WIDTH
    both = jnp.concatenate(
        [jnp.where(low, x, 0.0), jnp.where(low, pltpu.roll(x, WIDTH, 1), 0.0)], axis=0
    ).astype(BF16)
    scores = dot_nt(both, kv[...])
    probs = jnp.exp(scores - jnp.max(scores, axis=1, keepdims=True))
    total = jnp.sum(probs, axis=1, keepdims=True)
    mixed = dot(probs.astype(BF16), kv[...]) * (1.0 / total)
    half = x.shape[0]
    packed = jnp.where(low, pltpu.roll(mixed[0:half], WIDTH, 1), mixed[half:])
    out[...] = packed.reshape(out.shape).astype(BF16)


def coarse_attention(q, kv):
    vmem = pl.BlockSpec(memory_space=pltpu.VMEM)
    return pl.pallas_call(
        coarse_kernel,
        in_specs=[vmem, vmem],
        out_shape=jax.ShapeDtypeStruct(q.shape, BF16),
        compiler_params=pltpu.CompilerParams(vmem_limit_bytes=32 * MIB),
        cost_estimate=pl.CostEstimate(
            flops=8 * 10**9, bytes_accessed=16 * MIB, transcendentals=1 << 19
        ),
        name="coarse",
    )(q, kv)


def final_kernel(back, wout, mid, out, lifted):
    step = pl.program_id(0)

    @pl.when(step == 0)
    def _():
        low = lax.broadcasted_iota(jnp.int32, (8, 128), 1) < WIDTH
        top, bottom = [], []
        for pair in range(HEADS // 2):
            a = back[2 * pair].astype(F32)
            b = back[2 * pair + 1].astype(F32)
            top.append(jnp.where(low, a, pltpu.roll(b, WIDTH, 1)))
            bottom.append(jnp.where(low, pltpu.roll(a, WIDTH, 1), b))
        rows = [jnp.concatenate(top, axis=1), jnp.concatenate(bottom, axis=1)]
        lifted[...] = dot(jnp.concatenate(rows, axis=0).astype(BF16), wout[...])

    each = mid.shape[0] // POOL
    for r in range(each):
        s = slice(r * POOL, (r + 1) * POOL)
        add = lifted[pl.ds(step * each + r, 1), :]
        out[s, :] = (mid[s, :].astype(F32) + add).astype(BF16)


def finish(back, wout, mid):
    rows = mid.shape[0]
    whole = lambda shape: pl.BlockSpec(shape, lambda g: (0,) * len(shape))
    return pl.pallas_call(
        final_kernel,
        grid=(rows // SUB,),
        in_specs=[
            whole(back.shape),
            whole((D, D)),
            pl.BlockSpec((SUB, D), lambda g: (g, 0)),
        ],
        out_specs=pl.BlockSpec((SUB, D), lambda g: (g, 0)),
        out_shape=jax.ShapeDtypeStruct((rows, D), BF16),
        scratch_shapes=[pltpu.VMEM((16, D), F32)],
        compiler_params=pltpu.CompilerParams(vmem_limit_bytes=20 * MIB),
        name="finish",
    )(back, wout, mid)


def body(
    token_ids,
    bar_mask,
    embed,
    mask_embed,
    local_gain,
    local_query,
    local_key,
    local_value,
    local_out,
    coarse_gain,
    coarse_query,
    coarse_key,
    coarse_value,
    coarse_out,
):
    rows = token_ids.shape[0]
    own = jnp.where(bar_mask == 1, VOCAB + 1, token_ids + 1)
    count = lax.axis_size(ALL)
    forward = [(i, i + 1) for i in range(count - 1)]
    backward = [(b, a) for a, b in forward]
    low = lax.ppermute(own[rows - HALF_WIN :], ALL, forward)
    high = lax.ppermute(own[:HALF_WIN], ALL, backward)
    att, payload = local_attention(
        low, own, high, mask_embed, local_gain, coarse_gain, embed,
        local_query, local_key, local_value, local_out, coarse_query, coarse_key, coarse_value,
    )
    got = lax.all_to_all(payload, PLANE, split_axis=0, concat_axis=0, tiled=True)
    q = got[:, 16:24]
    kv = got[:, 0:16].reshape(1, HEADS * 16, 128)
    peers = lax.axis_size(RING)
    kv = jnp.broadcast_to(kv, (peers,) + kv.shape[1:])
    kv = lax.all_to_all(kv, RING, split_axis=0, concat_axis=0, tiled=True)
    mid = make_mid(own, att, embed, mask_embed, local_out)
    kv, mid = lax.optimization_barrier((kv, mid))
    mixed = coarse_attention(q, kv.reshape(peers * HEADS * 16, 128))
    back = lax.all_to_all(mixed, PLANE, split_axis=0, concat_axis=0, tiled=True)
    return finish(back, coarse_out, mid)


def solution(mesh):
    fine = Mesh(mesh.devices.reshape((2,) * len(ALL)), ALL)
    placed = (P(ALL),) * 2 + (P(),) * 12
    return jax.shard_map(
        body, mesh=fine, in_specs=placed, out_specs=P(ALL, None), check_vma=False
    )
```

```python
import functools
import math

import jax
import jax.numpy as jnp
from jax import lax
from jax.experimental import pallas as pl
from jax.experimental.pallas import tpu as pltpu
from jax.sharding import Mesh
from jax.sharding import PartitionSpec as P

D = 1024
HEADS = 16
WIDTH = 64
VOCAB = 512
ROWS = VOCAB + 16
HALF_WIN = 512
POOL = 64
TILE = 512
SUB = 256
CHUNK = 48
GROUP = 4
COLS = GROUP * WIDTH
VROWS = WIDTH + 16
MIB = 1 << 20
ALL = ("x_hi", "x_lo", "y_hi", "z_hi", "z_lo", "y_lo", "core")
RING = ("z_hi", "z_lo", "core")
PLANE = ("x_hi", "x_lo", "y_hi", "y_lo")
F32 = jnp.float32
BF16 = jnp.bfloat16


def dot(a, b):
    return jnp.dot(a, b, preferred_element_type=F32)


def dot_nt(a, b):
    return lax.dot_general(a, b, (((1,), (1,)), ((), ())), preferred_element_type=F32)


def dot_tn(a, b):
    return lax.dot_general(a, b, (((0,), (0,)), ((), ())), preferred_element_type=F32)


def normalize(rows, gain):
    wide = rows.astype(F32)
    scaled = wide * lax.rsqrt(jnp.mean(wide * wide, axis=-1, keepdims=True) + 1e-05)
    return (scaled * gain.astype(F32)).astype(BF16)


def rounded(x):
    return x.astype(BF16).astype(F32)


def chunks(rows):
    return [slice(c, min(c + CHUNK, rows)) for c in range(0, rows, CHUNK)]


def fill_one_hot(out, first, ids):
    count = ids.shape[1]
    for s in chunks(ROWS):
        event = lax.broadcasted_iota(jnp.int32, (s.stop - s.start, count), 0) + (s.start + 1)
        out[s, first : first + count] = jnp.where(event == ids, 1.0, 0.0).astype(BF16)


def one_hot(ids):
    event = lax.broadcasted_iota(jnp.int32, (ROWS, ids.shape[1]), 0) + 1
    return jnp.where(event == ids, 1.0, 0.0).astype(BF16)


def local_kernel(
    low, own, high, mask_embed, gain, cgain, embed_hbm, lq, lk, lv, wout_hbm, cq, ck, cv,
    att, payload,
    hot, logs, scores, probs, pooled_in, matt, embed, local_w, weights, normed, k3, vt, att_out,
    sem_e, sem_l, sem_w, sem_o,
):
    step = pl.program_id(0)
    rows = att.shape[0]
    steps = HEADS // GROUP
    embed_copy = pltpu.make_async_copy(embed_hbm, embed, sem_e)

    def local_copy(i, g):
        src = (lq, lk, lv)[i].at[:, pl.ds(pl.multiple_of(g * COLS, COLS), COLS)]
        return pltpu.make_async_copy(src, local_w.at[i, g], sem_l.at[i, g])

    late_copies = [
        pltpu.make_async_copy(src, weights.at[i], sem_w.at[i])
        for i, src in enumerate((wout_hbm, cq, ck, cv))
    ]

    def out_copy(g):
        dst = att.at[:, pl.ds(pl.multiple_of(g * COLS, COLS), COLS)]
        return pltpu.make_async_copy(att_out.at[g], dst, sem_o.at[g])

    @pl.when(step == 0)
    def _():
        embed_copy.start()
        for g in range(steps):
            for i in range(3):
                local_copy(i, g).start()
        for copy in late_copies:
            copy.start()
        fill_one_hot(hot, 0, low[...].reshape(1, HALF_WIN))
        for c in range(0, rows, HALF_WIN):
            part = own[c : c + HALF_WIN].reshape(1, HALF_WIN)
            fill_one_hot(hot, HALF_WIN + c, part)
        fill_one_hot(hot, HALF_WIN + rows, high[...].reshape(1, HALF_WIN))
        j = lax.broadcasted_iota(jnp.int32, (SUB, SUB), 0)
        i = lax.broadcasted_iota(jnp.int32, (SUB, SUB), 1)
        first = jnp.where(j >= i, 1.0, 0.0).astype(BF16)
        last = jnp.where(j <= i, 1.0, 0.0).astype(BF16)
        every = jnp.ones((SUB, SUB), BF16)
        span = 2 * HALF_WIN // SUB
        for t in range(rows // SUB):
            block = lambda b: hot[:, (t + b) * SUB : (t + b + 1) * SUB]
            inner = block(1)
            for b in range(2, span):
                inner = inner + block(b)
            count = dot(block(0), first) + dot(inner, every) + dot(block(span), last)
            for s in chunks(ROWS):
                c = count[s]
                logs[s, t * SUB : (t + 1) * SUB] = jnp.where(
                    c > 0.0, jnp.log(jnp.maximum(c, 1.0)) * math.log2(math.e), -1e30
                )
        row = lax.broadcasted_iota(jnp.int32, (16, rows), 0)
        col = lax.broadcasted_iota(jnp.int32, (16, rows), 1)
        member = jnp.where(col // POOL == row, 1.0 / POOL, 0.0).astype(BF16)
        share = dot_nt(member, hot[:, HALF_WIN : HALF_WIN + rows])
        embed_copy.wait()
        mask_row = mask_embed[...].reshape(1, D)
        gain_row = gain[...].reshape(1, D)
        pooled_in[...] = dot(share[:, 0:VOCAB].astype(BF16), embed[...]) + share[
            :, VOCAB : VOCAB + 1
        ] * mask_row.astype(F32)
        for c in range(0, VOCAB, 32):
            normed[c : c + 32, :] = normalize(embed[c : c + 32], gain_row)
        keep = lax.broadcasted_iota(jnp.int32, (16, D), 0) == 0
        row = jnp.broadcast_to(normalize(mask_row, gain_row).astype(F32), (16, D))
        normed[VOCAB:ROWS, :] = jnp.where(keep, row, 0.0).astype(BF16)

    for i in range(3):
        local_copy(i, step).wait()
    q = rounded(dot(normed[...], local_w[0, step]))
    qt = q[0:VOCAB].T.astype(BF16)
    qm = jnp.broadcast_to(q[VOCAB : VOCAB + 1], (128, COLS)).T
    k_all = dot(normed[...], local_w[1, step])
    for c in chunks(ROWS):
        k = rounded(k_all[c]) * (math.log2(math.e) * WIDTH**-0.5)
        k_a = k.astype(BF16)
        rest = k - k_a.astype(F32)
        k_b = rest.astype(BF16)
        k_c = (rest - k_b.astype(F32)).astype(BF16)
        for h in range(GROUP):
            s = slice(h * WIDTH, (h + 1) * WIDTH)
            k3[h, c] = jnp.concatenate([k_a[:, s], k_b[:, s], k_c[:, s]], axis=1)
    v = rounded(dot(normed[...], local_w[2, step]))
    v_t = v[0:VOCAB].T
    v_m = jnp.broadcast_to(v[VOCAB : VOCAB + 1], (128, COLS)).T
    ones = jnp.where(lax.broadcasted_iota(jnp.int32, (16, VOCAB), 0) == 0, 1.0, 0.0)
    vm = []
    for h in range(GROUP):
        s = slice(h * WIDTH, (h + 1) * WIDTH)
        vt[h] = jnp.concatenate([v_t[s], ones], axis=0).astype(BF16)
        vm.append(jnp.concatenate([v_m[s], ones[:, 0:128]], axis=0))

    queries = []
    for t in range(rows // TILE):
        own_cols = slice(HALF_WIN + t * TILE, HALF_WIN + (t + 1) * TILE)
        masked = hot[VOCAB:ROWS, own_cols].astype(F32)[0:1]
        x = dot(qt, hot[0:VOCAB, own_cols])
        x = x + jnp.concatenate([qm] * (TILE // 128), axis=1) * masked
        queries.append(x.astype(BF16))

    units = [(t, h) for t in range(rows // TILE) for h in range(GROUP)]

    def score(u):
        t, h = units[u]
        q_h = queries[t][h * WIDTH : (h + 1) * WIDTH]
        s = dot(k3[h], jnp.concatenate([q_h, q_h, q_h], axis=0))
        top = None
        for c in chunks(ROWS):
            part = s[c] + logs[c, t * TILE : (t + 1) * TILE]
            scores[u % 2, c] = part
            peak = jnp.max(part.reshape((c.stop - c.start) // 8, 8, TILE), axis=0)
            top = peak if top is None else jnp.maximum(top, peak)
        return jnp.max(top, axis=0, keepdims=True)

    def mix(u, top):
        h = units[u][1]
        for c in chunks(ROWS):
            probs[u % 2, c] = jnp.exp2((scores[u % 2, c] - top).astype(BF16))
        mixed = dot(vt[h], probs[u % 2, 0:VOCAB])
        last = probs[u % 2, VOCAB:ROWS].astype(F32)[0:1]
        mixed = mixed + jnp.concatenate([vm[h]] * (TILE // 128), axis=1) * last
        return mixed[0:WIDTH] * (1.0 / mixed[WIDTH : WIDTH + 1])

    top = score(0)
    held = None
    for u, (t, h) in enumerate(units):
        later = score(u + 1) if u + 1 < len(units) else None
        mixed = mix(u, top)
        top = later
        if h % 2 == 0:
            held = mixed
            continue
        out = jnp.concatenate([held, mixed], axis=0).T
        cols = slice((h - 1) * WIDTH, (h + 1) * WIDTH)
        att_out[step, t * TILE : (t + 1) * TILE, cols] = out.astype(BF16)
        each = TILE // POOL
        mean = jnp.sum(out.reshape(each, POOL, 128), axis=1) * (1.0 / POOL)
        matt[step, t * each : (t + 1) * each, cols] = mean
    out_copy(step).start()

    @pl.when(step == steps - 1)
    def _():
        for copy in late_copies:
            copy.wait()
        mean = jnp.concatenate([matt[g] for g in range(steps)], axis=1)
        head = mean.astype(BF16)
        tail = (mean - head.astype(F32)).astype(BF16)
        lifted = dot(jnp.concatenate([head, tail], axis=0), weights[0])
        pooled = (pooled_in[...] + lifted[0:16] + lifted[16:32]).astype(BF16)
        coarse = normalize(pooled, cgain[...].reshape(1, D))
        q = rounded(dot(coarse, weights[1]))
        k = rounded(dot(coarse, weights[2]))
        v = rounded(dot(coarse, weights[3]))
        for h in range(HEADS):
            s = slice(h * WIDTH, (h + 1) * WIDTH)
            kv = jnp.concatenate([k[:, s], v[:, s]], axis=1)
            qq = jnp.concatenate([q[0:8, s], q[8:16, s]], axis=1)
            payload[h] = jnp.concatenate([kv, qq], axis=0).astype(BF16)
        for g in range(steps):
            out_copy(g).wait()


def local_attention(low, own, high, mask_embed, gain, cgain, *arrays):
    steps = HEADS // GROUP
    rows = own.shape[0]
    whole = lambda shape: pl.BlockSpec(shape, lambda g: (0,) * len(shape))
    hbm = pl.BlockSpec(memory_space=pl.ANY)
    small = (low, own, high, mask_embed, gain, cgain)
    return pl.pallas_call(
        local_kernel,
        grid=(steps,),
        in_specs=[whole(x.shape) for x in small] + [hbm] * len(arrays),
        out_specs=[hbm, whole((HEADS, 24, 128))],
        out_shape=[
            jax.ShapeDtypeStruct((rows, D), BF16),
            jax.ShapeDtypeStruct((HEADS, 24, 128), BF16),
        ],
        scratch_shapes=[
            pltpu.VMEM((ROWS, rows + 2 * HALF_WIN), BF16),
            pltpu.VMEM((ROWS, rows), F32),
            pltpu.VMEM((2, ROWS, TILE), F32),
            pltpu.VMEM((2, ROWS, TILE), BF16),
            pltpu.VMEM((16, D), F32),
            pltpu.VMEM((steps, rows // POOL, COLS), F32),
            pltpu.VMEM((VOCAB, D), BF16),
            pltpu.VMEM((3, steps, D, COLS), BF16),
            pltpu.VMEM((4, D, D), BF16),
            pltpu.VMEM((ROWS, D), BF16),
            pltpu.VMEM((GROUP, ROWS, 3 * WIDTH), BF16),
            pltpu.VMEM((GROUP, VROWS, VOCAB), BF16),
            pltpu.VMEM((steps, rows, COLS), BF16),
            pltpu.SemaphoreType.DMA(()),
            pltpu.SemaphoreType.DMA((3, steps)),
            pltpu.SemaphoreType.DMA((4,)),
            pltpu.SemaphoreType.DMA((steps,)),
        ],
        compiler_params=pltpu.CompilerParams(vmem_limit_bytes=60 * MIB),
        cost_estimate=pl.CostEstimate(
            flops=16 * rows * ROWS * D, bytes_accessed=20 * MIB, transcendentals=rows * ROWS * HEADS
        ),
        name="local",
    )(*small, *arrays)


def mid_kernel(ids, att, embed, mask_embed, wout, mid):
    hot = one_hot(ids[...].reshape(1, SUB))
    total = dot(att[...], wout[...]) + dot_tn(hot[0:VOCAB], embed[...])
    row = jnp.broadcast_to(mask_embed[...].reshape(1, D), (16, D))
    total = total + dot_tn(hot[VOCAB:ROWS], row)
    mid[...] = total.astype(BF16)


def make_mid(ids, att, embed, mask_embed, wout):
    rows = att.shape[0]
    whole = lambda shape: pl.BlockSpec(shape, lambda g: (0,) * len(shape))
    return pl.pallas_call(
        mid_kernel,
        grid=(rows // SUB,),
        in_specs=[
            pl.BlockSpec((SUB,), lambda g: (g,)),
            pl.BlockSpec((SUB, D), lambda g: (g, 0)),
            whole((VOCAB, D)),
            whole((D,)),
            whole((D, D)),
        ],
        out_specs=pl.BlockSpec((SUB, D), lambda g: (g, 0)),
        out_shape=jax.ShapeDtypeStruct((rows, D), BF16),
        compiler_params=pltpu.CompilerParams(vmem_limit_bytes=60 * MIB),
        cost_estimate=pl.CostEstimate(
            flops=2 * rows * (ROWS + D) * D, bytes_accessed=8 * MIB, transcendentals=0
        ),
        name="mid",
    )(ids, att, embed, mask_embed, wout)


def coarse_kernel(q, kv, out):
    x = q[...].astype(F32).reshape(q.shape[0] * 8, 128) * WIDTH**-0.5
    low = lax.broadcasted_iota(jnp.int32, x.shape, 1) < WIDTH
    both = jnp.concatenate(
        [jnp.where(low, x, 0.0), jnp.where(low, pltpu.roll(x, WIDTH, 1), 0.0)], axis=0
    ).astype(BF16)
    scores = dot_nt(both, kv[...])
    probs = jnp.exp(scores - jnp.max(scores, axis=1, keepdims=True))
    total = jnp.sum(probs, axis=1, keepdims=True)
    mixed = dot(probs.astype(BF16), kv[...]) * (1.0 / total)
    half = x.shape[0]
    packed = jnp.where(low, pltpu.roll(mixed[0:half], WIDTH, 1), mixed[half:])
    out[...] = packed.reshape(out.shape).astype(BF16)


def coarse_attention(q, kv):
    vmem = pl.BlockSpec(memory_space=pltpu.VMEM)
    return pl.pallas_call(
        coarse_kernel,
        in_specs=[vmem, vmem],
        out_shape=jax.ShapeDtypeStruct(q.shape, BF16),
        compiler_params=pltpu.CompilerParams(vmem_limit_bytes=32 * MIB),
        cost_estimate=pl.CostEstimate(
            flops=8 * 10**9, bytes_accessed=16 * MIB, transcendentals=1 << 19
        ),
        name="coarse",
    )(q, kv)


def final_kernel(back, wout, mid, out, lifted):
    step = pl.program_id(0)

    @pl.when(step == 0)
    def _():
        low = lax.broadcasted_iota(jnp.int32, (8, 128), 1) < WIDTH
        top, bottom = [], []
        for pair in range(HEADS // 2):
            a = back[2 * pair].astype(F32)
            b = back[2 * pair + 1].astype(F32)
            top.append(jnp.where(low, a, pltpu.roll(b, WIDTH, 1)))
            bottom.append(jnp.where(low, pltpu.roll(a, WIDTH, 1), b))
        rows = [jnp.concatenate(top, axis=1), jnp.concatenate(bottom, axis=1)]
        lifted[...] = dot(jnp.concatenate(rows, axis=0).astype(BF16), wout[...])

    each = mid.shape[0] // POOL
    for r in range(each):
        s = slice(r * POOL, (r + 1) * POOL)
        add = lifted[pl.ds(step * each + r, 1), :]
        out[s, :] = (mid[s, :].astype(F32) + add).astype(BF16)


def finish(back, wout, mid):
    rows = mid.shape[0]
    whole = lambda shape: pl.BlockSpec(shape, lambda g: (0,) * len(shape))
    return pl.pallas_call(
        final_kernel,
        grid=(rows // SUB,),
        in_specs=[
            whole(back.shape),
            whole((D, D)),
            pl.BlockSpec((SUB, D), lambda g: (g, 0)),
        ],
        out_specs=pl.BlockSpec((SUB, D), lambda g: (g, 0)),
        out_shape=jax.ShapeDtypeStruct((rows, D), BF16),
        scratch_shapes=[pltpu.VMEM((16, D), F32)],
        compiler_params=pltpu.CompilerParams(vmem_limit_bytes=20 * MIB),
        name="finish",
    )(back, wout, mid)


def body(
    token_ids,
    bar_mask,
    embed,
    mask_embed,
    local_gain,
    local_query,
    local_key,
    local_value,
    local_out,
    coarse_gain,
    coarse_query,
    coarse_key,
    coarse_value,
    coarse_out,
):
    rows = token_ids.shape[0]
    own = jnp.where(bar_mask == 1, VOCAB + 1, token_ids + 1)
    count = lax.axis_size(ALL)
    forward = [(i, i + 1) for i in range(count - 1)]
    backward = [(b, a) for a, b in forward]
    low = lax.ppermute(own[rows - HALF_WIN :], ALL, forward)
    high = lax.ppermute(own[:HALF_WIN], ALL, backward)
    att, payload = local_attention(
        low, own, high, mask_embed, local_gain, coarse_gain, embed,
        local_query, local_key, local_value, local_out, coarse_query, coarse_key, coarse_value,
    )
    got = lax.all_to_all(payload, PLANE, split_axis=0, concat_axis=0, tiled=True)
    q = got[:, 16:24]
    kv = got[:, 0:16].reshape(1, HEADS * 16, 128)
    peers = lax.axis_size(RING)
    kv = jnp.broadcast_to(kv, (peers,) + kv.shape[1:])
    kv = lax.all_to_all(kv, RING, split_axis=0, concat_axis=0, tiled=True)
    mid = make_mid(own, att, embed, mask_embed, local_out)
    kv, mid = lax.optimization_barrier((kv, mid))
    mixed = coarse_attention(q, kv.reshape(peers * HEADS * 16, 128))
    back = lax.all_to_all(mixed, PLANE, split_axis=0, concat_axis=0, tiled=True)
    return finish(back, coarse_out, mid)


def solution(mesh):
    fine = Mesh(mesh.devices.reshape((2,) * len(ALL)), ALL)
    placed = (P(ALL),) * 2 + (P(),) * 12
    return jax.shard_map(
        body, mesh=fine, in_specs=placed, out_specs=P(ALL, None), check_vma=False
    )
```

```python
import functools
import math

import jax
import jax.numpy as jnp
from jax import lax
from jax.experimental import pallas as pl
from jax.experimental.pallas import tpu as pltpu
from jax.sharding import Mesh
from jax.sharding import PartitionSpec as P

D = 1024
HEADS = 16
WIDTH = 64
VOCAB = 512
ROWS = VOCAB + 16
HALF_WIN = 512
POOL = 64
TILE = 512
SUB = 256
CHUNK = 48
GROUP = 4
COLS = GROUP * WIDTH
VROWS = WIDTH + 16
MIB = 1 << 20
ALL = ("x_hi", "x_lo", "y_hi", "z_hi", "z_lo", "y_lo", "core")
RING = ("z_hi", "z_lo", "core")
PLANE = ("x_hi", "x_lo", "y_hi", "y_lo")
F32 = jnp.float32
BF16 = jnp.bfloat16


def dot(a, b):
    return jnp.dot(a, b, preferred_element_type=F32)


def dot_nt(a, b):
    return lax.dot_general(a, b, (((1,), (1,)), ((), ())), preferred_element_type=F32)


def dot_tn(a, b):
    return lax.dot_general(a, b, (((0,), (0,)), ((), ())), preferred_element_type=F32)


def normalize(rows, gain):
    wide = rows.astype(F32)
    scaled = wide * lax.rsqrt(jnp.mean(wide * wide, axis=-1, keepdims=True) + 1e-05)
    return (scaled * gain.astype(F32)).astype(BF16)


def rounded(x):
    return x.astype(BF16).astype(F32)


def chunks(rows):
    return [slice(c, min(c + CHUNK, rows)) for c in range(0, rows, CHUNK)]


def fill_one_hot(out, first, ids):
    count = ids.shape[1]
    for s in chunks(ROWS):
        event = lax.broadcasted_iota(jnp.int32, (s.stop - s.start, count), 0) + (s.start + 1)
        out[s, first : first + count] = jnp.where(event == ids, 1.0, 0.0).astype(BF16)


def one_hot(ids):
    event = lax.broadcasted_iota(jnp.int32, (ROWS, ids.shape[1]), 0) + 1
    return jnp.where(event == ids, 1.0, 0.0).astype(BF16)


def local_kernel(
    low, own, high, mask_embed, gain, cgain, embed_hbm, lq, lk, lv, wout_hbm, cq, ck, cv,
    att, payload,
    hot, logs, scores, probs, pooled_in, matt, embed, local_w, weights, normed, k2, vt, att_out,
    sem_e, sem_l, sem_w, sem_o,
):
    step = pl.program_id(0)
    rows = att.shape[0]
    steps = HEADS // GROUP
    embed_copy = pltpu.make_async_copy(embed_hbm, embed, sem_e)

    def local_copy(i, g):
        src = (lq, lk, lv)[i].at[:, pl.ds(pl.multiple_of(g * COLS, COLS), COLS)]
        return pltpu.make_async_copy(src, local_w.at[i, g], sem_l.at[i, g])

    late_copies = [
        pltpu.make_async_copy(src, weights.at[i], sem_w.at[i])
        for i, src in enumerate((wout_hbm, cq, ck, cv))
    ]

    def out_copy(g):
        dst = att.at[:, pl.ds(pl.multiple_of(g * COLS, COLS), COLS)]
        return pltpu.make_async_copy(att_out.at[g], dst, sem_o.at[g])

    @pl.when(step == 0)
    def _():
        embed_copy.start()
        for g in range(steps):
            for i in range(3):
                local_copy(i, g).start()
        for copy in late_copies:
            copy.start()
        fill_one_hot(hot, 0, low[...].reshape(1, HALF_WIN))
        for c in range(0, rows, HALF_WIN):
            part = own[c : c + HALF_WIN].reshape(1, HALF_WIN)
            fill_one_hot(hot, HALF_WIN + c, part)
        fill_one_hot(hot, HALF_WIN + rows, high[...].reshape(1, HALF_WIN))
        j = lax.broadcasted_iota(jnp.int32, (SUB, SUB), 0)
        i = lax.broadcasted_iota(jnp.int32, (SUB, SUB), 1)
        first = jnp.where(j >= i, 1.0, 0.0).astype(BF16)
        last = jnp.where(j <= i, 1.0, 0.0).astype(BF16)
        every = jnp.ones((SUB, SUB), BF16)
        span = 2 * HALF_WIN // SUB
        for t in range(rows // SUB):
            block = lambda b: hot[:, (t + b) * SUB : (t + b + 1) * SUB]
            inner = block(1)
            for b in range(2, span):
                inner = inner + block(b)
            count = dot(block(0), first) + dot(inner, every) + dot(block(span), last)
            for s in chunks(ROWS):
                c = count[s]
                logs[s, t * SUB : (t + 1) * SUB] = jnp.where(
                    c > 0.0, jnp.log(jnp.maximum(c, 1.0)) * math.log2(math.e), -1e30
                )
        row = lax.broadcasted_iota(jnp.int32, (16, rows), 0)
        col = lax.broadcasted_iota(jnp.int32, (16, rows), 1)
        member = jnp.where(col // POOL == row, 1.0 / POOL, 0.0).astype(BF16)
        share = dot_nt(member, hot[:, HALF_WIN : HALF_WIN + rows])
        embed_copy.wait()
        mask_row = mask_embed[...].reshape(1, D)
        gain_row = gain[...].reshape(1, D)
        pooled_in[...] = dot(share[:, 0:VOCAB].astype(BF16), embed[...]) + share[
            :, VOCAB : VOCAB + 1
        ] * mask_row.astype(F32)
        for c in range(0, VOCAB, 32):
            normed[c : c + 32, :] = normalize(embed[c : c + 32], gain_row)
        keep = lax.broadcasted_iota(jnp.int32, (16, D), 0) == 0
        row = jnp.broadcast_to(normalize(mask_row, gain_row).astype(F32), (16, D))
        normed[VOCAB:ROWS, :] = jnp.where(keep, row, 0.0).astype(BF16)

    for i in range(3):
        local_copy(i, step).wait()
    q = rounded(dot(normed[...], local_w[0, step]))
    qt = q[0:VOCAB].T.astype(BF16)
    qm = jnp.broadcast_to(q[VOCAB : VOCAB + 1], (128, COLS)).T
    k_all = dot(normed[...], local_w[1, step])
    for c in chunks(ROWS):
        k = rounded(k_all[c]) * (math.log2(math.e) * WIDTH**-0.5)
        k_a = k.astype(BF16)
        k_b = (k - k_a.astype(F32)).astype(BF16)
        for h in range(GROUP):
            s = slice(h * WIDTH, (h + 1) * WIDTH)
            k2[h, c] = jnp.concatenate([k_a[:, s], k_b[:, s]], axis=1)
    v = rounded(dot(normed[...], local_w[2, step]))
    v_t = v[0:VOCAB].T
    v_m = jnp.broadcast_to(v[VOCAB : VOCAB + 1], (128, COLS)).T
    ones = jnp.where(lax.broadcasted_iota(jnp.int32, (16, VOCAB), 0) == 0, 1.0, 0.0)
    vm = []
    for h in range(GROUP):
        s = slice(h * WIDTH, (h + 1) * WIDTH)
        vt[h] = jnp.concatenate([v_t[s], ones], axis=0).astype(BF16)
        vm.append(jnp.concatenate([v_m[s], ones[:, 0:128]], axis=0))

    queries = []
    for t in range(rows // TILE):
        own_cols = slice(HALF_WIN + t * TILE, HALF_WIN + (t + 1) * TILE)
        masked = hot[VOCAB:ROWS, own_cols].astype(F32)[0:1]
        x = dot(qt, hot[0:VOCAB, own_cols])
        x = x + jnp.concatenate([qm] * (TILE // 128), axis=1) * masked
        queries.append(x.astype(BF16))

    units = [(t, h) for t in range(rows // TILE) for h in range(GROUP)]

    def score(u):
        t, h = units[u]
        q_h = queries[t][h * WIDTH : (h + 1) * WIDTH]
        s = dot(k2[h], jnp.concatenate([q_h, q_h], axis=0))
        top = None
        for c in chunks(ROWS):
            part = s[c] + logs[c, t * TILE : (t + 1) * TILE]
            scores[u % 2, c] = part
            peak = jnp.max(part.reshape((c.stop - c.start) // 8, 8, TILE), axis=0)
            top = peak if top is None else jnp.maximum(top, peak)
        return jnp.max(top, axis=0, keepdims=True)

    def mix(u, top):
        h = units[u][1]
        for c in chunks(ROWS):
            probs[u % 2, c] = jnp.exp2((scores[u % 2, c] - top).astype(BF16))
        mixed = dot(vt[h], probs[u % 2, 0:VOCAB])
        last = probs[u % 2, VOCAB:ROWS].astype(F32)[0:1]
        mixed = mixed + jnp.concatenate([vm[h]] * (TILE // 128), axis=1) * last
        return mixed[0:WIDTH] * (1.0 / mixed[WIDTH : WIDTH + 1])

    top = score(0)
    held = None
    for u, (t, h) in enumerate(units):
        later = score(u + 1) if u + 1 < len(units) else None
        mixed = mix(u, top)
        top = later
        if h % 2 == 0:
            held = mixed
            continue
        out = jnp.concatenate([held, mixed], axis=0).T
        cols = slice((h - 1) * WIDTH, (h + 1) * WIDTH)
        att_out[step, t * TILE : (t + 1) * TILE, cols] = out.astype(BF16)
        each = TILE // POOL
        mean = jnp.sum(out.reshape(each, POOL, 128), axis=1) * (1.0 / POOL)
        matt[step, t * each : (t + 1) * each, cols] = mean
    out_copy(step).start()

    @pl.when(step == steps - 1)
    def _():
        for copy in late_copies:
            copy.wait()
        mean = jnp.concatenate([matt[g] for g in range(steps)], axis=1)
        head = mean.astype(BF16)
        tail = (mean - head.astype(F32)).astype(BF16)
        lifted = dot(jnp.concatenate([head, tail], axis=0), weights[0])
        pooled = (pooled_in[...] + lifted[0:16] + lifted[16:32]).astype(BF16)
        coarse = normalize(pooled, cgain[...].reshape(1, D))
        q = rounded(dot(coarse, weights[1]))
        k = rounded(dot(coarse, weights[2]))
        v = rounded(dot(coarse, weights[3]))
        for h in range(HEADS):
            s = slice(h * WIDTH, (h + 1) * WIDTH)
            kv = jnp.concatenate([k[:, s], v[:, s]], axis=1)
            qq = jnp.concatenate([q[0:8, s], q[8:16, s]], axis=1)
            payload[h] = jnp.concatenate([kv, qq], axis=0).astype(BF16)
        for g in range(steps):
            out_copy(g).wait()


def local_attention(low, own, high, mask_embed, gain, cgain, *arrays):
    steps = HEADS // GROUP
    rows = own.shape[0]
    whole = lambda shape: pl.BlockSpec(shape, lambda g: (0,) * len(shape))
    hbm = pl.BlockSpec(memory_space=pl.ANY)
    small = (low, own, high, mask_embed, gain, cgain)
    return pl.pallas_call(
        local_kernel,
        grid=(steps,),
        in_specs=[whole(x.shape) for x in small] + [hbm] * len(arrays),
        out_specs=[hbm, whole((HEADS, 24, 128))],
        out_shape=[
            jax.ShapeDtypeStruct((rows, D), BF16),
            jax.ShapeDtypeStruct((HEADS, 24, 128), BF16),
        ],
        scratch_shapes=[
            pltpu.VMEM((ROWS, rows + 2 * HALF_WIN), BF16),
            pltpu.VMEM((ROWS, rows), F32),
            pltpu.VMEM((2, ROWS, TILE), F32),
            pltpu.VMEM((2, ROWS, TILE), BF16),
            pltpu.VMEM((16, D), F32),
            pltpu.VMEM((steps, rows // POOL, COLS), F32),
            pltpu.VMEM((VOCAB, D), BF16),
            pltpu.VMEM((3, steps, D, COLS), BF16),
            pltpu.VMEM((4, D, D), BF16),
            pltpu.VMEM((ROWS, D), BF16),
            pltpu.VMEM((GROUP, ROWS, 2 * WIDTH), BF16),
            pltpu.VMEM((GROUP, VROWS, VOCAB), BF16),
            pltpu.VMEM((steps, rows, COLS), BF16),
            pltpu.SemaphoreType.DMA(()),
            pltpu.SemaphoreType.DMA((3, steps)),
            pltpu.SemaphoreType.DMA((4,)),
            pltpu.SemaphoreType.DMA((steps,)),
        ],
        compiler_params=pltpu.CompilerParams(vmem_limit_bytes=60 * MIB),
        cost_estimate=pl.CostEstimate(
            flops=16 * rows * ROWS * D, bytes_accessed=20 * MIB, transcendentals=rows * ROWS * HEADS
        ),
        name="local",
    )(*small, *arrays)


def mid_kernel(ids, att, embed, mask_embed, wout, mid):
    hot = one_hot(ids[...].reshape(1, SUB))
    total = dot(att[...], wout[...]) + dot_tn(hot[0:VOCAB], embed[...])
    row = jnp.broadcast_to(mask_embed[...].reshape(1, D), (16, D))
    total = total + dot_tn(hot[VOCAB:ROWS], row)
    mid[...] = total.astype(BF16)


def make_mid(ids, att, embed, mask_embed, wout):
    rows = att.shape[0]
    whole = lambda shape: pl.BlockSpec(shape, lambda g: (0,) * len(shape))
    return pl.pallas_call(
        mid_kernel,
        grid=(rows // SUB,),
        in_specs=[
            pl.BlockSpec((SUB,), lambda g: (g,)),
            pl.BlockSpec((SUB, D), lambda g: (g, 0)),
            whole((VOCAB, D)),
            whole((D,)),
            whole((D, D)),
        ],
        out_specs=pl.BlockSpec((SUB, D), lambda g: (g, 0)),
        out_shape=jax.ShapeDtypeStruct((rows, D), BF16),
        compiler_params=pltpu.CompilerParams(vmem_limit_bytes=60 * MIB),
        cost_estimate=pl.CostEstimate(
            flops=2 * rows * (ROWS + D) * D, bytes_accessed=8 * MIB, transcendentals=0
        ),
        name="mid",
    )(ids, att, embed, mask_embed, wout)


def coarse_kernel(q, kv, out):
    x = q[...].astype(F32).reshape(q.shape[0] * 8, 128) * WIDTH**-0.5
    low = lax.broadcasted_iota(jnp.int32, x.shape, 1) < WIDTH
    both = jnp.concatenate(
        [jnp.where(low, x, 0.0), jnp.where(low, pltpu.roll(x, WIDTH, 1), 0.0)], axis=0
    ).astype(BF16)
    scores = dot_nt(both, kv[...])
    probs = jnp.exp(scores - jnp.max(scores, axis=1, keepdims=True))
    total = jnp.sum(probs, axis=1, keepdims=True)
    mixed = dot(probs.astype(BF16), kv[...]) * (1.0 / total)
    half = x.shape[0]
    packed = jnp.where(low, pltpu.roll(mixed[0:half], WIDTH, 1), mixed[half:])
    out[...] = packed.reshape(out.shape).astype(BF16)


def coarse_attention(q, kv):
    vmem = pl.BlockSpec(memory_space=pltpu.VMEM)
    return pl.pallas_call(
        coarse_kernel,
        in_specs=[vmem, vmem],
        out_shape=jax.ShapeDtypeStruct(q.shape, BF16),
        compiler_params=pltpu.CompilerParams(vmem_limit_bytes=32 * MIB),
        cost_estimate=pl.CostEstimate(
            flops=8 * 10**9, bytes_accessed=16 * MIB, transcendentals=1 << 19
        ),
        name="coarse",
    )(q, kv)


def final_kernel(back, wout, mid, out, lifted):
    step = pl.program_id(0)

    @pl.when(step == 0)
    def _():
        low = lax.broadcasted_iota(jnp.int32, (8, 128), 1) < WIDTH
        top, bottom = [], []
        for pair in range(HEADS // 2):
            a = back[2 * pair].astype(F32)
            b = back[2 * pair + 1].astype(F32)
            top.append(jnp.where(low, a, pltpu.roll(b, WIDTH, 1)))
            bottom.append(jnp.where(low, pltpu.roll(a, WIDTH, 1), b))
        rows = [jnp.concatenate(top, axis=1), jnp.concatenate(bottom, axis=1)]
        lifted[...] = dot(jnp.concatenate(rows, axis=0).astype(BF16), wout[...])

    each = mid.shape[0] // POOL
    for r in range(each):
        s = slice(r * POOL, (r + 1) * POOL)
        add = lifted[pl.ds(step * each + r, 1), :]
        out[s, :] = (mid[s, :].astype(F32) + add).astype(BF16)


def finish(back, wout, mid):
    rows = mid.shape[0]
    whole = lambda shape: pl.BlockSpec(shape, lambda g: (0,) * len(shape))
    return pl.pallas_call(
        final_kernel,
        grid=(rows // SUB,),
        in_specs=[
            whole(back.shape),
            whole((D, D)),
            pl.BlockSpec((SUB, D), lambda g: (g, 0)),
        ],
        out_specs=pl.BlockSpec((SUB, D), lambda g: (g, 0)),
        out_shape=jax.ShapeDtypeStruct((rows, D), BF16),
        scratch_shapes=[pltpu.VMEM((16, D), F32)],
        compiler_params=pltpu.CompilerParams(vmem_limit_bytes=20 * MIB),
        name="finish",
    )(back, wout, mid)


def body(
    token_ids,
    bar_mask,
    embed,
    mask_embed,
    local_gain,
    local_query,
    local_key,
    local_value,
    local_out,
    coarse_gain,
    coarse_query,
    coarse_key,
    coarse_value,
    coarse_out,
):
    rows = token_ids.shape[0]
    own = jnp.where(bar_mask == 1, VOCAB + 1, token_ids + 1)
    count = lax.axis_size(ALL)
    forward = [(i, i + 1) for i in range(count - 1)]
    backward = [(b, a) for a, b in forward]
    low = lax.ppermute(own[rows - HALF_WIN :], ALL, forward)
    high = lax.ppermute(own[:HALF_WIN], ALL, backward)
    att, payload = local_attention(
        low, own, high, mask_embed, local_gain, coarse_gain, embed,
        local_query, local_key, local_value, local_out, coarse_query, coarse_key, coarse_value,
    )
    got = lax.all_to_all(payload, PLANE, split_axis=0, concat_axis=0, tiled=True)
    q = got[:, 16:24]
    kv = got[:, 0:16].reshape(1, HEADS * 16, 128)
    peers = lax.axis_size(RING)
    kv = jnp.broadcast_to(kv, (peers,) + kv.shape[1:])
    kv = lax.all_to_all(kv, RING, split_axis=0, concat_axis=0, tiled=True)
    mid = make_mid(own, att, embed, mask_embed, local_out)
    kv, mid = lax.optimization_barrier((kv, mid))
    mixed = coarse_attention(q, kv.reshape(peers * HEADS * 16, 128))
    back = lax.all_to_all(mixed, PLANE, split_axis=0, concat_axis=0, tiled=True)
    return finish(back, coarse_out, mid)


def solution(mesh):
    fine = Mesh(mesh.devices.reshape((2,) * len(ALL)), ALL)
    placed = (P(ALL),) * 2 + (P(),) * 12
    return jax.shard_map(
        body, mesh=fine, in_specs=placed, out_specs=P(ALL, None), check_vma=False
    )
```

```python
import functools
import math

import jax
import jax.numpy as jnp
from jax import lax
from jax.experimental import pallas as pl
from jax.experimental.pallas import tpu as pltpu
from jax.sharding import Mesh
from jax.sharding import PartitionSpec as P

D = 1024
HEADS = 16
WIDTH = 64
VOCAB = 512
ROWS = VOCAB + 16
HALF_WIN = 512
POOL = 64
TILE = 512
SUB = 256
CHUNK = 48
GROUP = 8
COLS = GROUP * WIDTH
VROWS = WIDTH + 16
MIB = 1 << 20
ALL = ("x_hi", "x_lo", "y_hi", "z_hi", "z_lo", "y_lo", "core")
RING = ("z_hi", "z_lo", "core")
PLANE = ("x_hi", "x_lo", "y_hi", "y_lo")
F32 = jnp.float32
BF16 = jnp.bfloat16


def dot(a, b):
    return jnp.dot(a, b, preferred_element_type=F32)


def dot_nt(a, b):
    return lax.dot_general(a, b, (((1,), (1,)), ((), ())), preferred_element_type=F32)


def dot_tn(a, b):
    return lax.dot_general(a, b, (((0,), (0,)), ((), ())), preferred_element_type=F32)


def normalize(rows, gain):
    wide = rows.astype(F32)
    scaled = wide * lax.rsqrt(jnp.mean(wide * wide, axis=-1, keepdims=True) + 1e-05)
    return (scaled * gain.astype(F32)).astype(BF16)


def rounded(x):
    return x.astype(BF16).astype(F32)


def chunks(rows):
    return [slice(c, min(c + CHUNK, rows)) for c in range(0, rows, CHUNK)]


def fill_one_hot(out, first, ids):
    count = ids.shape[1]
    for s in chunks(ROWS):
        event = lax.broadcasted_iota(jnp.int32, (s.stop - s.start, count), 0) + (s.start + 1)
        out[s, first : first + count] = jnp.where(event == ids, 1.0, 0.0).astype(BF16)


def one_hot(ids):
    event = lax.broadcasted_iota(jnp.int32, (ROWS, ids.shape[1]), 0) + 1
    return jnp.where(event == ids, 1.0, 0.0).astype(BF16)


def local_kernel(
    low, own, high, mask_embed, gain, cgain, embed_hbm, lq, lk, lv, wout_hbm, cq, ck, cv,
    att, payload,
    hot, logs, scores, probs, pooled_in, matt, embed, local_w, weights, normed, k2, vt, att_out,
    sem_e, sem_l, sem_w, sem_o,
):
    step = pl.program_id(0)
    rows = att.shape[0]
    steps = HEADS // GROUP
    embed_copy = pltpu.make_async_copy(embed_hbm, embed, sem_e)

    def local_copy(i, g):
        src = (lq, lk, lv)[i].at[:, pl.ds(pl.multiple_of(g * COLS, COLS), COLS)]
        return pltpu.make_async_copy(src, local_w.at[i, g], sem_l.at[i, g])

    late_copies = [
        pltpu.make_async_copy(src, weights.at[i], sem_w.at[i])
        for i, src in enumerate((wout_hbm, cq, ck, cv))
    ]

    def out_copy(g):
        dst = att.at[:, pl.ds(pl.multiple_of(g * COLS, COLS), COLS)]
        return pltpu.make_async_copy(att_out.at[g], dst, sem_o.at[g])

    @pl.when(step == 0)
    def _():
        embed_copy.start()
        for g in range(steps):
            for i in range(3):
                local_copy(i, g).start()
        for copy in late_copies:
            copy.start()
        fill_one_hot(hot, 0, low[...].reshape(1, HALF_WIN))
        for c in range(0, rows, HALF_WIN):
            part = own[c : c + HALF_WIN].reshape(1, HALF_WIN)
            fill_one_hot(hot, HALF_WIN + c, part)
        fill_one_hot(hot, HALF_WIN + rows, high[...].reshape(1, HALF_WIN))
        j = lax.broadcasted_iota(jnp.int32, (SUB, SUB), 0)
        i = lax.broadcasted_iota(jnp.int32, (SUB, SUB), 1)
        first = jnp.where(j >= i, 1.0, 0.0).astype(BF16)
        last = jnp.where(j <= i, 1.0, 0.0).astype(BF16)
        every = jnp.ones((SUB, SUB), BF16)
        span = 2 * HALF_WIN // SUB
        for t in range(rows // SUB):
            block = lambda b: hot[:, (t + b) * SUB : (t + b + 1) * SUB]
            inner = block(1)
            for b in range(2, span):
                inner = inner + block(b)
            count = dot(block(0), first) + dot(inner, every) + dot(block(span), last)
            for s in chunks(ROWS):
                c = count[s]
                logs[s, t * SUB : (t + 1) * SUB] = jnp.where(
                    c > 0.0, jnp.log(jnp.maximum(c, 1.0)) * math.log2(math.e), -1e30
                )
        row = lax.broadcasted_iota(jnp.int32, (16, rows), 0)
        col = lax.broadcasted_iota(jnp.int32, (16, rows), 1)
        member = jnp.where(col // POOL == row, 1.0 / POOL, 0.0).astype(BF16)
        share = dot_nt(member, hot[:, HALF_WIN : HALF_WIN + rows])
        embed_copy.wait()
        mask_row = mask_embed[...].reshape(1, D)
        gain_row = gain[...].reshape(1, D)
        pooled_in[...] = dot(share[:, 0:VOCAB].astype(BF16), embed[...]) + share[
            :, VOCAB : VOCAB + 1
        ] * mask_row.astype(F32)
        for c in range(0, VOCAB, 32):
            normed[c : c + 32, :] = normalize(embed[c : c + 32], gain_row)
        keep = lax.broadcasted_iota(jnp.int32, (16, D), 0) == 0
        row = jnp.broadcast_to(normalize(mask_row, gain_row).astype(F32), (16, D))
        normed[VOCAB:ROWS, :] = jnp.where(keep, row, 0.0).astype(BF16)

    local_copy(0, step).wait()
    q = rounded(dot(normed[...], local_w[0, step]))
    qt = q[0:VOCAB].T.astype(BF16)
    qm = jnp.broadcast_to(q[VOCAB : VOCAB + 1], (128, COLS)).T
    local_copy(1, step).wait()
    k_all = dot(normed[...], local_w[1, step])
    for c in chunks(ROWS):
        k = rounded(k_all[c]) * (math.log2(math.e) * WIDTH**-0.5)
        k_a = k.astype(BF16)
        k_b = (k - k_a.astype(F32)).astype(BF16)
        for h in range(GROUP):
            s = slice(h * WIDTH, (h + 1) * WIDTH)
            k2[h, c] = jnp.concatenate([k_a[:, s], k_b[:, s]], axis=1)
    local_copy(2, step).wait()
    v = rounded(dot(normed[...], local_w[2, step]))
    v_t = v[0:VOCAB].T
    v_m = jnp.broadcast_to(v[VOCAB : VOCAB + 1], (128, COLS)).T
    ones = jnp.where(lax.broadcasted_iota(jnp.int32, (16, VOCAB), 0) == 0, 1.0, 0.0)
    vm = []
    for h in range(GROUP):
        s = slice(h * WIDTH, (h + 1) * WIDTH)
        vt[h] = jnp.concatenate([v_t[s], ones], axis=0).astype(BF16)
        vm.append(jnp.concatenate([v_m[s], ones[:, 0:128]], axis=0))

    queries = []
    for t in range(rows // TILE):
        own_cols = slice(HALF_WIN + t * TILE, HALF_WIN + (t + 1) * TILE)
        masked = hot[VOCAB:ROWS, own_cols].astype(F32)[0:1]
        x = dot(qt, hot[0:VOCAB, own_cols])
        x = x + jnp.concatenate([qm] * (TILE // 128), axis=1) * masked
        queries.append(x.astype(BF16))

    units = [(t, h) for t in range(rows // TILE) for h in range(GROUP)]

    def score(u):
        t, h = units[u]
        q_h = queries[t][h * WIDTH : (h + 1) * WIDTH]
        s = dot(k2[h], jnp.concatenate([q_h, q_h], axis=0))
        top = None
        for c in chunks(ROWS):
            part = s[c] + logs[c, t * TILE : (t + 1) * TILE]
            scores[u % 2, c] = part
            peak = jnp.max(part.reshape((c.stop - c.start) // 8, 8, TILE), axis=0)
            top = peak if top is None else jnp.maximum(top, peak)
        return jnp.max(top, axis=0, keepdims=True)

    def mix(u, top):
        h = units[u][1]
        for c in chunks(ROWS):
            probs[u % 2, c] = jnp.exp2((scores[u % 2, c] - top).astype(BF16))
        mixed = dot(vt[h], probs[u % 2, 0:VOCAB])
        last = probs[u % 2, VOCAB:ROWS].astype(F32)[0:1]
        mixed = mixed + jnp.concatenate([vm[h]] * (TILE // 128), axis=1) * last
        return mixed[0:WIDTH] * (1.0 / mixed[WIDTH : WIDTH + 1])

    top = score(0)
    held = None
    for u, (t, h) in enumerate(units):
        later = score(u + 1) if u + 1 < len(units) else None
        mixed = mix(u, top)
        top = later
        if h % 2 == 0:
            held = mixed
            continue
        out = jnp.concatenate([held, mixed], axis=0).T
        cols = slice((h - 1) * WIDTH, (h + 1) * WIDTH)
        att_out[step, t * TILE : (t + 1) * TILE, cols] = out.astype(BF16)
        each = TILE // POOL
        mean = jnp.sum(out.reshape(each, POOL, 128), axis=1) * (1.0 / POOL)
        matt[step, t * each : (t + 1) * each, cols] = mean
    out_copy(step).start()

    @pl.when(step == steps - 1)
    def _():
        for copy in late_copies:
            copy.wait()
        mean = jnp.concatenate([matt[g] for g in range(steps)], axis=1)
        head = mean.astype(BF16)
        tail = (mean - head.astype(F32)).astype(BF16)
        lifted = dot(jnp.concatenate([head, tail], axis=0), weights[0])
        pooled = (pooled_in[...] + lifted[0:16] + lifted[16:32]).astype(BF16)
        coarse = normalize(pooled, cgain[...].reshape(1, D))
        q = rounded(dot(coarse, weights[1]))
        k = rounded(dot(coarse, weights[2]))
        v = rounded(dot(coarse, weights[3]))
        for h in range(HEADS):
            s = slice(h * WIDTH, (h + 1) * WIDTH)
            kv = jnp.concatenate([k[:, s], v[:, s]], axis=1)
            qq = jnp.concatenate([q[0:8, s], q[8:16, s]], axis=1)
            payload[h] = jnp.concatenate([kv, qq], axis=0).astype(BF16)
        for g in range(steps):
            out_copy(g).wait()


def local_attention(low, own, high, mask_embed, gain, cgain, *arrays):
    steps = HEADS // GROUP
    rows = own.shape[0]
    whole = lambda shape: pl.BlockSpec(shape, lambda g: (0,) * len(shape))
    hbm = pl.BlockSpec(memory_space=pl.ANY)
    small = (low, own, high, mask_embed, gain, cgain)
    return pl.pallas_call(
        local_kernel,
        grid=(steps,),
        in_specs=[whole(x.shape) for x in small] + [hbm] * len(arrays),
        out_specs=[hbm, whole((HEADS, 24, 128))],
        out_shape=[
            jax.ShapeDtypeStruct((rows, D), BF16),
            jax.ShapeDtypeStruct((HEADS, 24, 128), BF16),
        ],
        scratch_shapes=[
            pltpu.VMEM((ROWS, rows + 2 * HALF_WIN), BF16),
            pltpu.VMEM((ROWS, rows), F32),
            pltpu.VMEM((2, ROWS, TILE), F32),
            pltpu.VMEM((2, ROWS, TILE), BF16),
            pltpu.VMEM((16, D), F32),
            pltpu.VMEM((steps, rows // POOL, COLS), F32),
            pltpu.VMEM((VOCAB, D), BF16),
            pltpu.VMEM((3, steps, D, COLS), BF16),
            pltpu.VMEM((4, D, D), BF16),
            pltpu.VMEM((ROWS, D), BF16),
            pltpu.VMEM((GROUP, ROWS, 2 * WIDTH), BF16),
            pltpu.VMEM((GROUP, VROWS, VOCAB), BF16),
            pltpu.VMEM((steps, rows, COLS), BF16),
            pltpu.SemaphoreType.DMA(()),
            pltpu.SemaphoreType.DMA((3, steps)),
            pltpu.SemaphoreType.DMA((4,)),
            pltpu.SemaphoreType.DMA((steps,)),
        ],
        compiler_params=pltpu.CompilerParams(vmem_limit_bytes=60 * MIB),
        cost_estimate=pl.CostEstimate(
            flops=16 * rows * ROWS * D, bytes_accessed=20 * MIB, transcendentals=rows * ROWS * HEADS
        ),
        name="local",
    )(*small, *arrays)


def mid_kernel(ids, att, embed, mask_embed, wout, mid):
    hot = one_hot(ids[...].reshape(1, SUB))
    total = dot(att[...], wout[...]) + dot_tn(hot[0:VOCAB], embed[...])
    row = jnp.broadcast_to(mask_embed[...].reshape(1, D), (16, D))
    total = total + dot_tn(hot[VOCAB:ROWS], row)
    mid[...] = total.astype(BF16)


def make_mid(ids, att, embed, mask_embed, wout):
    rows = att.shape[0]
    whole = lambda shape: pl.BlockSpec(shape, lambda g: (0,) * len(shape))
    return pl.pallas_call(
        mid_kernel,
        grid=(rows // SUB,),
        in_specs=[
            pl.BlockSpec((SUB,), lambda g: (g,)),
            pl.BlockSpec((SUB, D), lambda g: (g, 0)),
            whole((VOCAB, D)),
            whole((D,)),
            whole((D, D)),
        ],
        out_specs=pl.BlockSpec((SUB, D), lambda g: (g, 0)),
        out_shape=jax.ShapeDtypeStruct((rows, D), BF16),
        compiler_params=pltpu.CompilerParams(vmem_limit_bytes=60 * MIB),
        cost_estimate=pl.CostEstimate(
            flops=2 * rows * (ROWS + D) * D, bytes_accessed=8 * MIB, transcendentals=0
        ),
        name="mid",
    )(ids, att, embed, mask_embed, wout)


def coarse_kernel(q, kv, out):
    x = q[...].astype(F32).reshape(q.shape[0] * 8, 128) * WIDTH**-0.5
    low = lax.broadcasted_iota(jnp.int32, x.shape, 1) < WIDTH
    both = jnp.concatenate(
        [jnp.where(low, x, 0.0), jnp.where(low, pltpu.roll(x, WIDTH, 1), 0.0)], axis=0
    ).astype(BF16)
    scores = dot_nt(both, kv[...])
    probs = jnp.exp(scores - jnp.max(scores, axis=1, keepdims=True))
    total = jnp.sum(probs, axis=1, keepdims=True)
    mixed = dot(probs.astype(BF16), kv[...]) * (1.0 / total)
    half = x.shape[0]
    packed = jnp.where(low, pltpu.roll(mixed[0:half], WIDTH, 1), mixed[half:])
    out[...] = packed.reshape(out.shape).astype(BF16)


def coarse_attention(q, kv):
    vmem = pl.BlockSpec(memory_space=pltpu.VMEM)
    return pl.pallas_call(
        coarse_kernel,
        in_specs=[vmem, vmem],
        out_shape=jax.ShapeDtypeStruct(q.shape, BF16),
        compiler_params=pltpu.CompilerParams(vmem_limit_bytes=32 * MIB),
        cost_estimate=pl.CostEstimate(
            flops=8 * 10**9, bytes_accessed=16 * MIB, transcendentals=1 << 19
        ),
        name="coarse",
    )(q, kv)


def final_kernel(back, wout, mid, out, lifted):
    step = pl.program_id(0)

    @pl.when(step == 0)
    def _():
        low = lax.broadcasted_iota(jnp.int32, (8, 128), 1) < WIDTH
        top, bottom = [], []
        for pair in range(HEADS // 2):
            a = back[2 * pair].astype(F32)
            b = back[2 * pair + 1].astype(F32)
            top.append(jnp.where(low, a, pltpu.roll(b, WIDTH, 1)))
            bottom.append(jnp.where(low, pltpu.roll(a, WIDTH, 1), b))
        rows = [jnp.concatenate(top, axis=1), jnp.concatenate(bottom, axis=1)]
        lifted[...] = dot(jnp.concatenate(rows, axis=0).astype(BF16), wout[...])

    each = mid.shape[0] // POOL
    for r in range(each):
        s = slice(r * POOL, (r + 1) * POOL)
        add = lifted[pl.ds(step * each + r, 1), :]
        out[s, :] = (mid[s, :].astype(F32) + add).astype(BF16)


def finish(back, wout, mid):
    rows = mid.shape[0]
    whole = lambda shape: pl.BlockSpec(shape, lambda g: (0,) * len(shape))
    return pl.pallas_call(
        final_kernel,
        grid=(rows // SUB,),
        in_specs=[
            whole(back.shape),
            whole((D, D)),
            pl.BlockSpec((SUB, D), lambda g: (g, 0)),
        ],
        out_specs=pl.BlockSpec((SUB, D), lambda g: (g, 0)),
        out_shape=jax.ShapeDtypeStruct((rows, D), BF16),
        scratch_shapes=[pltpu.VMEM((16, D), F32)],
        compiler_params=pltpu.CompilerParams(vmem_limit_bytes=20 * MIB),
        name="finish",
    )(back, wout, mid)


def body(
    token_ids,
    bar_mask,
    embed,
    mask_embed,
    local_gain,
    local_query,
    local_key,
    local_value,
    local_out,
    coarse_gain,
    coarse_query,
    coarse_key,
    coarse_value,
    coarse_out,
):
    rows = token_ids.shape[0]
    own = jnp.where(bar_mask == 1, VOCAB + 1, token_ids + 1)
    count = lax.axis_size(ALL)
    forward = [(i, i + 1) for i in range(count - 1)]
    backward = [(b, a) for a, b in forward]
    low = lax.ppermute(own[rows - HALF_WIN :], ALL, forward)
    high = lax.ppermute(own[:HALF_WIN], ALL, backward)
    att, payload = local_attention(
        low, own, high, mask_embed, local_gain, coarse_gain, embed,
        local_query, local_key, local_value, local_out, coarse_query, coarse_key, coarse_value,
    )
    got = lax.all_to_all(payload, PLANE, split_axis=0, concat_axis=0, tiled=True)
    q = got[:, 16:24]
    kv = got[:, 0:16].reshape(1, HEADS * 16, 128)
    peers = lax.axis_size(RING)
    kv = jnp.broadcast_to(kv, (peers,) + kv.shape[1:])
    kv = lax.all_to_all(kv, RING, split_axis=0, concat_axis=0, tiled=True)
    mid = make_mid(own, att, embed, mask_embed, local_out)
    kv, mid = lax.optimization_barrier((kv, mid))
    mixed = coarse_attention(q, kv.reshape(peers * HEADS * 16, 128))
    back = lax.all_to_all(mixed, PLANE, split_axis=0, concat_axis=0, tiled=True)
    return finish(back, coarse_out, mid)


def solution(mesh):
    fine = Mesh(mesh.devices.reshape((2,) * len(ALL)), ALL)
    placed = (P(ALL),) * 2 + (P(),) * 12
    return jax.shard_map(
        body, mesh=fine, in_specs=placed, out_specs=P(ALL, None), check_vma=False
    )
```

```python
import functools
import math

import jax
import jax.numpy as jnp
from jax import lax
from jax.experimental import pallas as pl
from jax.experimental.pallas import tpu as pltpu
from jax.sharding import Mesh
from jax.sharding import PartitionSpec as P

D = 1024
HEADS = 16
WIDTH = 64
VOCAB = 512
ROWS = VOCAB + 16
HALF_WIN = 512
POOL = 64
TILE = 1024
SUB = 256
CHUNK = 48
GROUP = 4
COLS = GROUP * WIDTH
VROWS = WIDTH + 16
MIB = 1 << 20
ALL = ("x_hi", "x_lo", "y_hi", "z_hi", "z_lo", "y_lo", "core")
RING = ("z_hi", "z_lo", "core")
PLANE = ("x_hi", "x_lo", "y_hi", "y_lo")
F32 = jnp.float32
BF16 = jnp.bfloat16


def dot(a, b):
    return jnp.dot(a, b, preferred_element_type=F32)


def dot_nt(a, b):
    return lax.dot_general(a, b, (((1,), (1,)), ((), ())), preferred_element_type=F32)


def dot_tn(a, b):
    return lax.dot_general(a, b, (((0,), (0,)), ((), ())), preferred_element_type=F32)


def normalize(rows, gain):
    wide = rows.astype(F32)
    scaled = wide * lax.rsqrt(jnp.mean(wide * wide, axis=-1, keepdims=True) + 1e-05)
    return (scaled * gain.astype(F32)).astype(BF16)


def rounded(x):
    return x.astype(BF16).astype(F32)


def chunks(rows):
    return [slice(c, min(c + CHUNK, rows)) for c in range(0, rows, CHUNK)]


def fill_one_hot(out, first, ids):
    count = ids.shape[1]
    for s in chunks(ROWS):
        event = lax.broadcasted_iota(jnp.int32, (s.stop - s.start, count), 0) + (s.start + 1)
        out[s, first : first + count] = jnp.where(event == ids, 1.0, 0.0).astype(BF16)


def one_hot(ids):
    event = lax.broadcasted_iota(jnp.int32, (ROWS, ids.shape[1]), 0) + 1
    return jnp.where(event == ids, 1.0, 0.0).astype(BF16)


def local_kernel(
    low, own, high, mask_embed, gain, cgain, embed_hbm, lq, lk, lv, wout_hbm, cq, ck, cv,
    att, payload,
    hot, logs, scores, probs, pooled_in, matt, embed, local_w, weights, normed, k2, vt, att_out, held, peak, vt_last, vm_last,
    sem_e, sem_l, sem_w, sem_o,
):
    step = pl.program_id(0)
    rows = att.shape[0]
    steps = HEADS // GROUP
    embed_copy = pltpu.make_async_copy(embed_hbm, embed, sem_e)

    def local_copy(i, g):
        src = (lq, lk, lv)[i].at[:, pl.ds(pl.multiple_of(g * COLS, COLS), COLS)]
        dst = local_w.at[g, :, i * COLS : (i + 1) * COLS]
        return pltpu.make_async_copy(src, dst, sem_l.at[i, g])

    late_copies = [
        pltpu.make_async_copy(src, weights.at[i], sem_w.at[i])
        for i, src in enumerate((wout_hbm, cq, ck, cv))
    ]

    def out_copy(g):
        dst = att.at[:, pl.ds(pl.multiple_of(g * COLS, COLS), COLS)]
        return pltpu.make_async_copy(att_out.at[g], dst, sem_o.at[g])

    @pl.when(step == 0)
    def _():
        embed_copy.start()
        for g in range(steps):
            for i in range(3):
                local_copy(i, g).start()
        for copy in late_copies:
            copy.start()
        fill_one_hot(hot, 0, low[...].reshape(1, HALF_WIN))
        for c in range(0, rows, HALF_WIN):
            part = own[c : c + HALF_WIN].reshape(1, HALF_WIN)
            fill_one_hot(hot, HALF_WIN + c, part)
        fill_one_hot(hot, HALF_WIN + rows, high[...].reshape(1, HALF_WIN))
        j = lax.broadcasted_iota(jnp.int32, (SUB, SUB), 0)
        i = lax.broadcasted_iota(jnp.int32, (SUB, SUB), 1)
        first = jnp.where(j >= i, 1.0, 0.0).astype(BF16)
        last = jnp.where(j <= i, 1.0, 0.0).astype(BF16)
        every = jnp.ones((SUB, SUB), BF16)
        span = 2 * HALF_WIN // SUB
        for t in range(rows // SUB):
            block = lambda b: hot[:, (t + b) * SUB : (t + b + 1) * SUB]
            inner = block(1)
            for b in range(2, span):
                inner = inner + block(b)
            count = dot(block(0), first) + dot(inner, every) + dot(block(span), last)
            for s in chunks(ROWS):
                c = count[s]
                logs[s, t * SUB : (t + 1) * SUB] = jnp.where(
                    c > 0.0, jnp.log(jnp.maximum(c, 1.0)) * math.log2(math.e), -1e30
                )
        row = lax.broadcasted_iota(jnp.int32, (16, rows), 0)
        col = lax.broadcasted_iota(jnp.int32, (16, rows), 1)
        member = jnp.where(col // POOL == row, 1.0 / POOL, 0.0).astype(BF16)
        share = dot_nt(member, hot[:, HALF_WIN : HALF_WIN + rows])
        embed_copy.wait()
        mask_row = mask_embed[...].reshape(1, D)
        gain_row = gain[...].reshape(1, D)
        pooled_in[...] = dot(share[:, 0:VOCAB].astype(BF16), embed[...]) + share[
            :, VOCAB : VOCAB + 1
        ] * mask_row.astype(F32)
        for c in range(0, VOCAB, 32):
            normed[c : c + 32, :] = normalize(embed[c : c + 32], gain_row)
        keep = lax.broadcasted_iota(jnp.int32, (16, D), 0) == 0
        row = jnp.broadcast_to(normalize(mask_row, gain_row).astype(F32), (16, D))
        normed[VOCAB:ROWS, :] = jnp.where(keep, row, 0.0).astype(BF16)

    for i in range(3):
        local_copy(i, step).wait()
    tables = dot(normed[...], local_w[step])

    def mix(vt_h, vm_h, slot, top):
        for c in chunks(ROWS):
            probs[slot, c] = jnp.exp2((scores[slot, c] - top).astype(BF16))
        mixed = dot(vt_h, probs[slot, 0:VOCAB])
        last = probs[slot, VOCAB:ROWS].astype(F32)[0:1]
        mixed = mixed + jnp.concatenate([vm_h] * (rows // 128), axis=1) * last
        return mixed[0:WIDTH] * (1.0 / mixed[WIDTH : WIDTH + 1])

    def put(group, pair, even, odd):
        out = jnp.concatenate([even, odd], axis=0).T
        cols = slice(pair * 2 * WIDTH, (pair + 1) * 2 * WIDTH)
        att_out[group, :, cols] = out.astype(BF16)
        matt[group, :, cols] = jnp.sum(out.reshape(rows // POOL, POOL, 128), axis=1) * (1.0 / POOL)

    def put_last(group):
        put(group, GROUP // 2 - 1, held[...], mix(vt_last[...], vm_last[...], 1, peak[0:1]))

    put_last(jnp.maximum(step - 1, 0))

    @pl.when(step > 0)
    def _():
        out_copy(step - 1).start()

    q = rounded(tables[:, 0:COLS])
    qt = q[0:VOCAB].T.astype(BF16)
    qm = jnp.broadcast_to(q[VOCAB : VOCAB + 1], (128, COLS)).T
    own_cols = slice(HALF_WIN, HALF_WIN + rows)
    masked = hot[VOCAB:ROWS, own_cols].astype(F32)[0:1]
    x = dot(qt, hot[0:VOCAB, own_cols])
    queries = (x + jnp.concatenate([qm] * (rows // 128), axis=1) * masked).astype(BF16)
    for c in chunks(ROWS):
        k = rounded(tables[c, COLS : 2 * COLS]) * (math.log2(math.e) * WIDTH**-0.5)
        k_a = k.astype(BF16)
        k_b = (k - k_a.astype(F32)).astype(BF16)
        for h in range(GROUP):
            s = slice(h * WIDTH, (h + 1) * WIDTH)
            k2[h, c] = jnp.concatenate([k_a[:, s], k_b[:, s]], axis=1)

    def score(h):
        q_h = queries[h * WIDTH : (h + 1) * WIDTH]
        s = dot(k2[h], jnp.concatenate([q_h, q_h], axis=0))
        top = None
        for c in chunks(ROWS):
            part = s[c] + logs[c]
            scores[h % 2, c] = part
            best = jnp.max(part.reshape((c.stop - c.start) // 8, 8, rows), axis=0)
            top = best if top is None else jnp.maximum(top, best)
        return jnp.max(top, axis=0, keepdims=True)

    top = score(0)
    v = rounded(tables[:, 2 * COLS :])
    v_t = v[0:VOCAB].T
    v_m = jnp.broadcast_to(v[VOCAB : VOCAB + 1], (128, COLS)).T
    ones = jnp.where(lax.broadcasted_iota(jnp.int32, (16, VOCAB), 0) == 0, 1.0, 0.0)
    vm = []
    for h in range(GROUP):
        s = slice(h * WIDTH, (h + 1) * WIDTH)
        vt[h] = jnp.concatenate([v_t[s], ones], axis=0).astype(BF16)
        vm.append(jnp.concatenate([v_m[s], ones[:, 0:128]], axis=0))

    even = None
    for h in range(GROUP - 1):
        later = score(h + 1)
        mixed = mix(vt[h], vm[h], h % 2, top)
        top = later
        if h % 2 == 0:
            even = mixed
        else:
            put(step, h // 2, even, mixed)
    held[...] = even
    peak[...] = jnp.broadcast_to(top, peak.shape)
    vt_last[...] = vt[GROUP - 1]
    vm_last[...] = vm[GROUP - 1]

    @pl.when(step == steps - 1)
    def _():
        put_last(step)
        out_copy(step).start()
        for copy in late_copies:
            copy.wait()
        mean = jnp.concatenate([matt[g] for g in range(steps)], axis=1)
        head = mean.astype(BF16)
        tail = (mean - head.astype(F32)).astype(BF16)
        lifted = dot(jnp.concatenate([head, tail], axis=0), weights[0])
        pooled = (pooled_in[...] + lifted[0:16] + lifted[16:32]).astype(BF16)
        coarse = normalize(pooled, cgain[...].reshape(1, D))
        q = rounded(dot(coarse, weights[1]))
        k = rounded(dot(coarse, weights[2]))
        v = rounded(dot(coarse, weights[3]))
        for h in range(HEADS):
            s = slice(h * WIDTH, (h + 1) * WIDTH)
            kv = jnp.concatenate([k[:, s], v[:, s]], axis=1)
            qq = jnp.concatenate([q[0:8, s], q[8:16, s]], axis=1)
            payload[h] = jnp.concatenate([kv, qq], axis=0).astype(BF16)
        for g in range(steps):
            out_copy(g).wait()


def local_attention(low, own, high, mask_embed, gain, cgain, *arrays):
    steps = HEADS // GROUP
    rows = own.shape[0]
    whole = lambda shape: pl.BlockSpec(shape, lambda g: (0,) * len(shape))
    hbm = pl.BlockSpec(memory_space=pl.ANY)
    small = (low, own, high, mask_embed, gain, cgain)
    return pl.pallas_call(
        local_kernel,
        grid=(steps,),
        in_specs=[whole(x.shape) for x in small] + [hbm] * len(arrays),
        out_specs=[hbm, whole((HEADS, 24, 128))],
        out_shape=[
            jax.ShapeDtypeStruct((rows, D), BF16),
            jax.ShapeDtypeStruct((HEADS, 24, 128), BF16),
        ],
        scratch_shapes=[
            pltpu.VMEM((ROWS, rows + 2 * HALF_WIN), BF16),
            pltpu.VMEM((ROWS, rows), F32),
            pltpu.VMEM((2, ROWS, TILE), F32),
            pltpu.VMEM((2, ROWS, TILE), BF16),
            pltpu.VMEM((16, D), F32),
            pltpu.VMEM((steps, rows // POOL, COLS), F32),
            pltpu.VMEM((VOCAB, D), BF16),
            pltpu.VMEM((steps, D, 3 * COLS), BF16),
            pltpu.VMEM((4, D, D), BF16),
            pltpu.VMEM((ROWS, D), BF16),
            pltpu.VMEM((GROUP, ROWS, 2 * WIDTH), BF16),
            pltpu.VMEM((GROUP, VROWS, VOCAB), BF16),
            pltpu.VMEM((steps, rows, COLS), BF16),
            pltpu.VMEM((WIDTH, rows), F32),
            pltpu.VMEM((8, rows), F32),
            pltpu.VMEM((VROWS, VOCAB), BF16),
            pltpu.VMEM((VROWS, 128), F32),
            pltpu.SemaphoreType.DMA(()),
            pltpu.SemaphoreType.DMA((3, steps)),
            pltpu.SemaphoreType.DMA((4,)),
            pltpu.SemaphoreType.DMA((steps,)),
        ],
        compiler_params=pltpu.CompilerParams(vmem_limit_bytes=60 * MIB),
        cost_estimate=pl.CostEstimate(
            flops=16 * rows * ROWS * D, bytes_accessed=20 * MIB, transcendentals=rows * ROWS * HEADS
        ),
        name="local",
    )(*small, *arrays)


def mid_kernel(ids, att, embed, mask_embed, wout, mid):
    hot = one_hot(ids[...].reshape(1, SUB))
    total = dot(att[...], wout[...]) + dot_tn(hot[0:VOCAB], embed[...])
    row = jnp.broadcast_to(mask_embed[...].reshape(1, D), (16, D))
    total = total + dot_tn(hot[VOCAB:ROWS], row)
    mid[...] = total.astype(BF16)


def make_mid(ids, att, embed, mask_embed, wout):
    rows = att.shape[0]
    whole = lambda shape: pl.BlockSpec(shape, lambda g: (0,) * len(shape))
    return pl.pallas_call(
        mid_kernel,
        grid=(rows // SUB,),
        in_specs=[
            pl.BlockSpec((SUB,), lambda g: (g,)),
            pl.BlockSpec((SUB, D), lambda g: (g, 0)),
            whole((VOCAB, D)),
            whole((D,)),
            whole((D, D)),
        ],
        out_specs=pl.BlockSpec((SUB, D), lambda g: (g, 0)),
        out_shape=jax.ShapeDtypeStruct((rows, D), BF16),
        compiler_params=pltpu.CompilerParams(vmem_limit_bytes=60 * MIB),
        cost_estimate=pl.CostEstimate(
            flops=2 * rows * (ROWS + D) * D, bytes_accessed=8 * MIB, transcendentals=0
        ),
        name="mid",
    )(ids, att, embed, mask_embed, wout)


def coarse_kernel(q, kv, out):
    x = q[...].astype(F32).reshape(q.shape[0] * 8, 128) * WIDTH**-0.5
    low = lax.broadcasted_iota(jnp.int32, x.shape, 1) < WIDTH
    both = jnp.concatenate(
        [jnp.where(low, x, 0.0), jnp.where(low, pltpu.roll(x, WIDTH, 1), 0.0)], axis=0
    ).astype(BF16)
    scores = dot_nt(both, kv[...])
    probs = jnp.exp(scores - jnp.max(scores, axis=1, keepdims=True))
    total = jnp.sum(probs, axis=1, keepdims=True)
    mixed = dot(probs.astype(BF16), kv[...]) * (1.0 / total)
    half = x.shape[0]
    packed = jnp.where(low, pltpu.roll(mixed[0:half], WIDTH, 1), mixed[half:])
    out[...] = packed.reshape(out.shape).astype(BF16)


def coarse_attention(q, kv):
    vmem = pl.BlockSpec(memory_space=pltpu.VMEM)
    return pl.pallas_call(
        coarse_kernel,
        in_specs=[vmem, vmem],
        out_shape=jax.ShapeDtypeStruct(q.shape, BF16),
        compiler_params=pltpu.CompilerParams(vmem_limit_bytes=32 * MIB),
        cost_estimate=pl.CostEstimate(
            flops=8 * 10**9, bytes_accessed=16 * MIB, transcendentals=1 << 19
        ),
        name="coarse",
    )(q, kv)


def final_kernel(back, wout, mid, out, lifted):
    step = pl.program_id(0)

    @pl.when(step == 0)
    def _():
        low = lax.broadcasted_iota(jnp.int32, (8, 128), 1) < WIDTH
        top, bottom = [], []
        for pair in range(HEADS // 2):
            a = back[2 * pair].astype(F32)
            b = back[2 * pair + 1].astype(F32)
            top.append(jnp.where(low, a, pltpu.roll(b, WIDTH, 1)))
            bottom.append(jnp.where(low, pltpu.roll(a, WIDTH, 1), b))
        rows = [jnp.concatenate(top, axis=1), jnp.concatenate(bottom, axis=1)]
        lifted[...] = dot(jnp.concatenate(rows, axis=0).astype(BF16), wout[...])

    each = mid.shape[0] // POOL
    for r in range(each):
        s = slice(r * POOL, (r + 1) * POOL)
        add = lifted[pl.ds(step * each + r, 1), :]
        out[s, :] = (mid[s, :].astype(F32) + add).astype(BF16)


def finish(back, wout, mid):
    rows = mid.shape[0]
    whole = lambda shape: pl.BlockSpec(shape, lambda g: (0,) * len(shape))
    return pl.pallas_call(
        final_kernel,
        grid=(rows // SUB,),
        in_specs=[
            whole(back.shape),
            whole((D, D)),
            pl.BlockSpec((SUB, D), lambda g: (g, 0)),
        ],
        out_specs=pl.BlockSpec((SUB, D), lambda g: (g, 0)),
        out_shape=jax.ShapeDtypeStruct((rows, D), BF16),
        scratch_shapes=[pltpu.VMEM((16, D), F32)],
        compiler_params=pltpu.CompilerParams(vmem_limit_bytes=20 * MIB),
        name="finish",
    )(back, wout, mid)


def body(
    token_ids,
    bar_mask,
    embed,
    mask_embed,
    local_gain,
    local_query,
    local_key,
    local_value,
    local_out,
    coarse_gain,
    coarse_query,
    coarse_key,
    coarse_value,
    coarse_out,
):
    rows = token_ids.shape[0]
    own = jnp.where(bar_mask == 1, VOCAB + 1, token_ids + 1)
    count = lax.axis_size(ALL)
    forward = [(i, i + 1) for i in range(count - 1)]
    backward = [(b, a) for a, b in forward]
    low = lax.ppermute(own[rows - HALF_WIN :], ALL, forward)
    high = lax.ppermute(own[:HALF_WIN], ALL, backward)
    att, payload = local_attention(
        low, own, high, mask_embed, local_gain, coarse_gain, embed,
        local_query, local_key, local_value, local_out, coarse_query, coarse_key, coarse_value,
    )
    got = lax.all_to_all(payload, PLANE, split_axis=0, concat_axis=0, tiled=True)
    q = got[:, 16:24]
    kv = got[:, 0:16].reshape(1, HEADS * 16, 128)
    peers = lax.axis_size(RING)
    kv = jnp.broadcast_to(kv, (peers,) + kv.shape[1:])
    kv = lax.all_to_all(kv, RING, split_axis=0, concat_axis=0, tiled=True)
    mid = make_mid(own, att, embed, mask_embed, local_out)
    kv, mid = lax.optimization_barrier((kv, mid))
    mixed = coarse_attention(q, kv.reshape(peers * HEADS * 16, 128))
    back = lax.all_to_all(mixed, PLANE, split_axis=0, concat_axis=0, tiled=True)
    return finish(back, coarse_out, mid)


def solution(mesh):
    fine = Mesh(mesh.devices.reshape((2,) * len(ALL)), ALL)
    placed = (P(ALL),) * 2 + (P(),) * 12
    return jax.shard_map(
        body, mesh=fine, in_specs=placed, out_specs=P(ALL, None), check_vma=False
    )
```

```python
import functools
import math

import jax
import jax.numpy as jnp
from jax import lax
from jax.experimental import pallas as pl
from jax.experimental.pallas import tpu as pltpu
from jax.sharding import Mesh
from jax.sharding import PartitionSpec as P

D = 1024
HEADS = 16
WIDTH = 64
VOCAB = 512
ROWS = VOCAB + 16
HALF_WIN = 512
POOL = 64
TILE = 512
SUB = 256
CHUNK = 48
GROUP = 4
COLS = GROUP * WIDTH
VROWS = WIDTH + 16
MIB = 1 << 20
ALL = ("x_hi", "x_lo", "y_hi", "z_hi", "z_lo", "y_lo", "core")
RING = ("z_hi", "z_lo", "core")
PLANE = ("x_hi", "x_lo", "y_hi", "y_lo")
F32 = jnp.float32
BF16 = jnp.bfloat16


def dot(a, b):
    return jnp.dot(a, b, preferred_element_type=F32)


def dot_nt(a, b):
    return lax.dot_general(a, b, (((1,), (1,)), ((), ())), preferred_element_type=F32)


def dot_tn(a, b):
    return lax.dot_general(a, b, (((0,), (0,)), ((), ())), preferred_element_type=F32)


def normalize(rows, gain):
    wide = rows.astype(F32)
    scaled = wide * lax.rsqrt(jnp.mean(wide * wide, axis=-1, keepdims=True) + 1e-05)
    return (scaled * gain.astype(F32)).astype(BF16)


def rounded(x):
    return x.astype(BF16).astype(F32)


def chunks(rows):
    return [slice(c, min(c + CHUNK, rows)) for c in range(0, rows, CHUNK)]


def fill_one_hot(out, first, ids):
    count = ids.shape[1]
    for s in chunks(ROWS):
        event = lax.broadcasted_iota(jnp.int32, (s.stop - s.start, count), 0) + (s.start + 1)
        out[s, first : first + count] = jnp.where(event == ids, 1.0, 0.0).astype(BF16)


def one_hot(ids):
    event = lax.broadcasted_iota(jnp.int32, (ROWS, ids.shape[1]), 0) + 1
    return jnp.where(event == ids, 1.0, 0.0).astype(BF16)


def local_kernel(
    low, own, high, mask_embed, gain, cgain, embed_hbm, lq, lk, lv, wout_hbm, cq, ck, cv,
    att, payload,
    hot, logs, scores, probs, pooled_in, matt, embed, local_w, weights, normed, k2, vt, att_out,
    sem_e, sem_l, sem_w, sem_o,
):
    step = pl.program_id(0)
    rows = att.shape[0]
    steps = HEADS // GROUP
    embed_copy = pltpu.make_async_copy(embed_hbm, embed, sem_e)

    def local_copy(i, g):
        src = (lq, lk, lv)[i].at[:, pl.ds(pl.multiple_of(g * COLS, COLS), COLS)]
        return pltpu.make_async_copy(src, local_w.at[i, g], sem_l.at[i, g])

    late_copies = [
        pltpu.make_async_copy(src, weights.at[i], sem_w.at[i])
        for i, src in enumerate((wout_hbm, cq, ck, cv))
    ]

    def out_copy(g):
        dst = att.at[:, pl.ds(pl.multiple_of(g * COLS, COLS), COLS)]
        return pltpu.make_async_copy(att_out.at[g], dst, sem_o.at[g])

    @pl.when(step == 0)
    def _():
        embed_copy.start()
        for g in range(steps):
            for i in range(3):
                local_copy(i, g).start()
        for copy in late_copies:
            copy.start()
        fill_one_hot(hot, 0, low[...].reshape(1, HALF_WIN))
        for c in range(0, rows, HALF_WIN):
            part = own[c : c + HALF_WIN].reshape(1, HALF_WIN)
            fill_one_hot(hot, HALF_WIN + c, part)
        fill_one_hot(hot, HALF_WIN + rows, high[...].reshape(1, HALF_WIN))
        j = lax.broadcasted_iota(jnp.int32, (SUB, SUB), 0)
        i = lax.broadcasted_iota(jnp.int32, (SUB, SUB), 1)
        first = jnp.where(j >= i, 1.0, 0.0).astype(BF16)
        last = jnp.where(j <= i, 1.0, 0.0).astype(BF16)
        every = jnp.ones((SUB, SUB), BF16)
        span = 2 * HALF_WIN // SUB
        for t in range(rows // SUB):
            block = lambda b: hot[:, (t + b) * SUB : (t + b + 1) * SUB]
            inner = block(1)
            for b in range(2, span):
                inner = inner + block(b)
            count = dot(block(0), first) + dot(inner, every) + dot(block(span), last)
            for s in chunks(ROWS):
                c = count[s]
                logs[s, t * SUB : (t + 1) * SUB] = jnp.where(
                    c > 0.0, jnp.log(jnp.maximum(c, 1.0)) * math.log2(math.e), -1e30
                )
        row = lax.broadcasted_iota(jnp.int32, (16, rows), 0)
        col = lax.broadcasted_iota(jnp.int32, (16, rows), 1)
        member = jnp.where(col // POOL == row, 1.0 / POOL, 0.0).astype(BF16)
        share = dot_nt(member, hot[:, HALF_WIN : HALF_WIN + rows])
        embed_copy.wait()
        mask_row = mask_embed[...].reshape(1, D)
        gain_row = gain[...].reshape(1, D)
        pooled_in[...] = dot(share[:, 0:VOCAB].astype(BF16), embed[...]) + share[
            :, VOCAB : VOCAB + 1
        ] * mask_row.astype(F32)
        for c in range(0, VOCAB, 32):
            normed[c : c + 32, :] = normalize(embed[c : c + 32], gain_row)
        keep = lax.broadcasted_iota(jnp.int32, (16, D), 0) == 0
        row = jnp.broadcast_to(normalize(mask_row, gain_row).astype(F32), (16, D))
        normed[VOCAB:ROWS, :] = jnp.where(keep, row, 0.0).astype(BF16)

    for i in range(3):
        local_copy(i, step).wait()
    q = rounded(dot(normed[...], local_w[0, step]))
    qt = q[0:VOCAB].T.astype(BF16)
    qm = jnp.broadcast_to(q[VOCAB : VOCAB + 1], (128, COLS)).T
    k_all = dot(normed[...], local_w[1, step])
    for c in chunks(ROWS):
        k = rounded(k_all[c]) * (math.log2(math.e) * WIDTH**-0.5)
        k_a = k.astype(BF16)
        k_b = (k - k_a.astype(F32)).astype(BF16)
        for h in range(GROUP):
            s = slice(h * WIDTH, (h + 1) * WIDTH)
            k2[h, c] = jnp.concatenate([k_a[:, s], k_b[:, s]], axis=1)
    v = rounded(dot(normed[...], local_w[2, step]))
    v_t = v[0:VOCAB].T
    v_m = jnp.broadcast_to(v[VOCAB : VOCAB + 1], (128, COLS)).T
    ones = jnp.where(lax.broadcasted_iota(jnp.int32, (16, VOCAB), 0) == 0, 1.0, 0.0)
    vm = []
    for h in range(GROUP):
        s = slice(h * WIDTH, (h + 1) * WIDTH)
        vt[h] = jnp.concatenate([v_t[s], ones], axis=0).astype(BF16)
        vm.append(jnp.concatenate([v_m[s], ones[:, 0:128]], axis=0))

    queries = []
    for t in range(rows // TILE):
        own_cols = slice(HALF_WIN + t * TILE, HALF_WIN + (t + 1) * TILE)
        masked = hot[VOCAB:ROWS, own_cols].astype(F32)[0:1]
        x = dot(qt, hot[0:VOCAB, own_cols])
        x = x + jnp.concatenate([qm] * (TILE // 128), axis=1) * masked
        queries.append(x.astype(BF16))

    units = [(t, h) for t in range(rows // TILE) for h in range(GROUP)]

    def score(u):
        t, h = units[u]
        q_h = queries[t][h * WIDTH : (h + 1) * WIDTH]
        s = dot(k2[h], jnp.concatenate([q_h, q_h], axis=0))
        top = None
        for c in chunks(ROWS):
            part = s[c] + logs[c, t * TILE : (t + 1) * TILE]
            scores[u % 2, c] = part
            peak = jnp.max(part.reshape((c.stop - c.start) // 8, 8, TILE), axis=0)
            top = peak if top is None else jnp.maximum(top, peak)
        return jnp.max(top, axis=0, keepdims=True)

    def mix(u, top):
        h = units[u][1]
        for c in chunks(ROWS):
            probs[u % 2, c] = jnp.exp2((scores[u % 2, c] - top).astype(BF16))
        mixed = dot(vt[h], probs[u % 2, 0:VOCAB])
        last = probs[u % 2, VOCAB:ROWS].astype(F32)[0:1]
        mixed = mixed + jnp.concatenate([vm[h]] * (TILE // 128), axis=1) * last
        return mixed[0:WIDTH] * (1.0 / mixed[WIDTH : WIDTH + 1])

    top = score(0)
    held = None
    for u, (t, h) in enumerate(units):
        later = score(u + 1) if u + 1 < len(units) else None
        mixed = mix(u, top)
        top = later
        if h % 2 == 0:
            held = mixed
            continue
        out = jnp.concatenate([held, mixed], axis=0).T
        cols = slice((h - 1) * WIDTH, (h + 1) * WIDTH)
        att_out[step, t * TILE : (t + 1) * TILE, cols] = out.astype(BF16)
        each = TILE // POOL
        mean = jnp.sum(out.reshape(each, POOL, 128), axis=1) * (1.0 / POOL)
        matt[step, t * each : (t + 1) * each, cols] = mean
    out_copy(step).start()

    @pl.when(step == steps - 1)
    def _():
        for copy in late_copies:
            copy.wait()
        mean = jnp.concatenate([matt[g] for g in range(steps)], axis=1)
        head = mean.astype(BF16)
        tail = (mean - head.astype(F32)).astype(BF16)
        lifted = dot(jnp.concatenate([head, tail], axis=0), weights[0])
        pooled = (pooled_in[...] + lifted[0:16] + lifted[16:32]).astype(BF16)
        coarse = normalize(pooled, cgain[...].reshape(1, D))
        q = rounded(dot(coarse, weights[1]))
        k = rounded(dot(coarse, weights[2]))
        v = rounded(dot(coarse, weights[3]))
        for h in range(HEADS):
            s = slice(h * WIDTH, (h + 1) * WIDTH)
            kv = jnp.concatenate([k[:, s], v[:, s]], axis=1)
            qq = jnp.concatenate([q[0:8, s], q[8:16, s]], axis=1)
            payload[h] = jnp.concatenate([kv, qq], axis=0).astype(BF16)
        for g in range(steps):
            out_copy(g).wait()


def local_attention(low, own, high, mask_embed, gain, cgain, *arrays):
    steps = HEADS // GROUP
    rows = own.shape[0]
    whole = lambda shape: pl.BlockSpec(shape, lambda g: (0,) * len(shape))
    hbm = pl.BlockSpec(memory_space=pl.ANY)
    small = (low, own, high, mask_embed, gain, cgain)
    return pl.pallas_call(
        local_kernel,
        grid=(steps,),
        in_specs=[whole(x.shape) for x in small] + [hbm] * len(arrays),
        out_specs=[hbm, whole((HEADS, 24, 128))],
        out_shape=[
            jax.ShapeDtypeStruct((rows, D), BF16),
            jax.ShapeDtypeStruct((HEADS, 24, 128), BF16),
        ],
        scratch_shapes=[
            pltpu.VMEM((ROWS, rows + 2 * HALF_WIN), BF16),
            pltpu.VMEM((ROWS, rows), F32),
            pltpu.VMEM((2, ROWS, TILE), F32),
            pltpu.VMEM((2, ROWS, TILE), BF16),
            pltpu.VMEM((16, D), F32),
            pltpu.VMEM((steps, rows // POOL, COLS), F32),
            pltpu.VMEM((VOCAB, D), BF16),
            pltpu.VMEM((3, steps, D, COLS), BF16),
            pltpu.VMEM((4, D, D), BF16),
            pltpu.VMEM((ROWS, D), BF16),
            pltpu.VMEM((GROUP, ROWS, 2 * WIDTH), BF16),
            pltpu.VMEM((GROUP, VROWS, VOCAB), BF16),
            pltpu.VMEM((steps, rows, COLS), BF16),
            pltpu.SemaphoreType.DMA(()),
            pltpu.SemaphoreType.DMA((3, steps)),
            pltpu.SemaphoreType.DMA((4,)),
            pltpu.SemaphoreType.DMA((steps,)),
        ],
        compiler_params=pltpu.CompilerParams(vmem_limit_bytes=60 * MIB),
        cost_estimate=pl.CostEstimate(
            flops=16 * rows * ROWS * D, bytes_accessed=20 * MIB, transcendentals=rows * ROWS * HEADS
        ),
        name="local",
    )(*small, *arrays)


def mid_kernel(ids, att, embed, mask_embed, wout, mid):
    hot = one_hot(ids[...].reshape(1, SUB))
    total = dot(att[...], wout[...]) + dot_tn(hot[0:VOCAB], embed[...])
    row = jnp.broadcast_to(mask_embed[...].reshape(1, D), (16, D))
    total = total + dot_tn(hot[VOCAB:ROWS], row)
    mid[...] = total.astype(BF16)


def make_mid(ids, att, embed, mask_embed, wout):
    rows = att.shape[0]
    whole = lambda shape: pl.BlockSpec(shape, lambda g: (0,) * len(shape))
    return pl.pallas_call(
        mid_kernel,
        grid=(rows // SUB,),
        in_specs=[
            pl.BlockSpec((SUB,), lambda g: (g,)),
            pl.BlockSpec((SUB, D), lambda g: (g, 0)),
            whole((VOCAB, D)),
            whole((D,)),
            whole((D, D)),
        ],
        out_specs=pl.BlockSpec((SUB, D), lambda g: (g, 0)),
        out_shape=jax.ShapeDtypeStruct((rows, D), BF16),
        compiler_params=pltpu.CompilerParams(vmem_limit_bytes=60 * MIB),
        cost_estimate=pl.CostEstimate(
            flops=2 * rows * (ROWS + D) * D, bytes_accessed=8 * MIB, transcendentals=0
        ),
        name="mid",
    )(ids, att, embed, mask_embed, wout)


def coarse_kernel(q, kv, out):
    x = q[...].astype(F32).reshape(q.shape[0] * 8, 128) * WIDTH**-0.5
    low = lax.broadcasted_iota(jnp.int32, x.shape, 1) < WIDTH
    both = jnp.concatenate(
        [jnp.where(low, x, 0.0), jnp.where(low, pltpu.roll(x, WIDTH, 1), 0.0)], axis=0
    ).astype(BF16)
    scores = dot_nt(both, kv[...])
    probs = jnp.exp(scores - jnp.max(scores, axis=1, keepdims=True))
    total = jnp.sum(probs, axis=1, keepdims=True)
    mixed = dot(probs.astype(BF16), kv[...]) * (1.0 / total)
    half = x.shape[0]
    packed = jnp.where(low, pltpu.roll(mixed[0:half], WIDTH, 1), mixed[half:])
    out[...] = packed.reshape(out.shape).astype(BF16)


def coarse_attention(q, kv):
    vmem = pl.BlockSpec(memory_space=pltpu.VMEM)
    return pl.pallas_call(
        coarse_kernel,
        in_specs=[vmem, vmem],
        out_shape=jax.ShapeDtypeStruct(q.shape, BF16),
        compiler_params=pltpu.CompilerParams(vmem_limit_bytes=32 * MIB),
        cost_estimate=pl.CostEstimate(
            flops=8 * 10**9, bytes_accessed=16 * MIB, transcendentals=1 << 19
        ),
        name="coarse",
    )(q, kv)


def final_kernel(back, wout, mid, out, lifted):
    step = pl.program_id(0)

    @pl.when(step == 0)
    def _():
        low = lax.broadcasted_iota(jnp.int32, (8, 128), 1) < WIDTH
        top, bottom = [], []
        for pair in range(HEADS // 2):
            a = back[2 * pair].astype(F32)
            b = back[2 * pair + 1].astype(F32)
            top.append(jnp.where(low, a, pltpu.roll(b, WIDTH, 1)))
            bottom.append(jnp.where(low, pltpu.roll(a, WIDTH, 1), b))
        rows = [jnp.concatenate(top, axis=1), jnp.concatenate(bottom, axis=1)]
        lifted[...] = dot(jnp.concatenate(rows, axis=0).astype(BF16), wout[...])

    each = mid.shape[0] // POOL
    for r in range(each):
        s = slice(r * POOL, (r + 1) * POOL)
        add = lifted[pl.ds(step * each + r, 1), :]
        out[s, :] = (mid[s, :].astype(F32) + add).astype(BF16)


def finish(back, wout, mid):
    rows = mid.shape[0]
    whole = lambda shape: pl.BlockSpec(shape, lambda g: (0,) * len(shape))
    return pl.pallas_call(
        final_kernel,
        grid=(rows // SUB,),
        in_specs=[
            whole(back.shape),
            whole((D, D)),
            pl.BlockSpec((SUB, D), lambda g: (g, 0)),
        ],
        out_specs=pl.BlockSpec((SUB, D), lambda g: (g, 0)),
        out_shape=jax.ShapeDtypeStruct((rows, D), BF16),
        scratch_shapes=[pltpu.VMEM((16, D), F32)],
        compiler_params=pltpu.CompilerParams(vmem_limit_bytes=20 * MIB),
        name="finish",
    )(back, wout, mid)


def body(
    token_ids,
    bar_mask,
    embed,
    mask_embed,
    local_gain,
    local_query,
    local_key,
    local_value,
    local_out,
    coarse_gain,
    coarse_query,
    coarse_key,
    coarse_value,
    coarse_out,
):
    rows = token_ids.shape[0]
    own = jnp.where(bar_mask == 1, VOCAB + 1, token_ids + 1)
    count = lax.axis_size(ALL)
    here = lax.axis_index(ALL)
    forward = [(i, (i + 1) % count) for i in range(count)]
    backward = [(b, a) for a, b in forward]
    low = lax.ppermute(jnp.where(here == count - 1, 0, own[rows - HALF_WIN :]), ALL, forward)
    high = lax.ppermute(jnp.where(here == 0, 0, own[:HALF_WIN]), ALL, backward)
    att, payload = local_attention(
        low, own, high, mask_embed, local_gain, coarse_gain, embed,
        local_query, local_key, local_value, local_out, coarse_query, coarse_key, coarse_value,
    )
    got = lax.all_to_all(payload, PLANE, split_axis=0, concat_axis=0, tiled=True)
    q = got[:, 16:24]
    kv = got[:, 0:16].reshape(1, HEADS * 16, 128)
    peers = lax.axis_size(RING)
    kv = jnp.broadcast_to(kv, (peers,) + kv.shape[1:])
    kv = lax.all_to_all(kv, RING, split_axis=0, concat_axis=0, tiled=True)
    mid = make_mid(own, att, embed, mask_embed, local_out)
    kv, mid = lax.optimization_barrier((kv, mid))
    mixed = coarse_attention(q, kv.reshape(peers * HEADS * 16, 128))
    back = lax.all_to_all(mixed, PLANE, split_axis=0, concat_axis=0, tiled=True)
    return finish(back, coarse_out, mid)


def solution(mesh):
    fine = Mesh(mesh.devices.reshape((2,) * len(ALL)), ALL)
    placed = (P(ALL),) * 2 + (P(),) * 12
    return jax.shard_map(
        body, mesh=fine, in_specs=placed, out_specs=P(ALL, None), check_vma=False
    )
```

```python
import functools
import math

import jax
import jax.numpy as jnp
from jax import lax
from jax.experimental import pallas as pl
from jax.experimental.pallas import tpu as pltpu
from jax.sharding import Mesh
from jax.sharding import PartitionSpec as P

D = 1024
HEADS = 16
WIDTH = 64
VOCAB = 512
ROWS = VOCAB + 16
HALF_WIN = 512
POOL = 64
TILE = 512
SUB = 256
CHUNK = 48
GROUP = 4
COLS = GROUP * WIDTH
VROWS = WIDTH + 16
MIB = 1 << 20
ALL = ("x_hi", "x_lo", "y_hi", "z_hi", "z_lo", "y_lo", "core")
RING = ("z_hi", "z_lo", "core")
PLANE = ("x_hi", "x_lo", "y_hi", "y_lo")
F32 = jnp.float32
BF16 = jnp.bfloat16


def dot(a, b):
    return jnp.dot(a, b, preferred_element_type=F32)


def dot_nt(a, b):
    return lax.dot_general(a, b, (((1,), (1,)), ((), ())), preferred_element_type=F32)


def dot_tn(a, b):
    return lax.dot_general(a, b, (((0,), (0,)), ((), ())), preferred_element_type=F32)


def normalize(rows, gain):
    wide = rows.astype(F32)
    scaled = wide * lax.rsqrt(jnp.mean(wide * wide, axis=-1, keepdims=True) + 1e-05)
    return (scaled * gain.astype(F32)).astype(BF16)


def rounded(x):
    return x.astype(BF16).astype(F32)


def chunks(rows):
    return [slice(c, min(c + CHUNK, rows)) for c in range(0, rows, CHUNK)]


def fill_one_hot(out, first, ids):
    count = ids.shape[1]
    for s in chunks(ROWS):
        event = lax.broadcasted_iota(jnp.int32, (s.stop - s.start, count), 0) + (s.start + 1)
        out[s, first : first + count] = jnp.where(event == ids, 1.0, 0.0).astype(BF16)


def one_hot(ids):
    event = lax.broadcasted_iota(jnp.int32, (ROWS, ids.shape[1]), 0) + 1
    return jnp.where(event == ids, 1.0, 0.0).astype(BF16)


def local_kernel(
    low, own, high, mask_embed, gain, cgain, embed_hbm, lq, lk, lv, wout_hbm, cq, ck, cv,
    att, payload,
    hot, logs, scores, probs, pooled_in, matt, embed, local_w, weights, normed, k2, vt, att_out,
    sem_e, sem_l, sem_w, sem_o,
):
    step = pl.program_id(0)
    rows = att.shape[0]
    steps = HEADS // GROUP
    embed_copy = pltpu.make_async_copy(embed_hbm, embed, sem_e)

    def local_copy(i, g):
        src = (lq, lk, lv)[i].at[:, pl.ds(pl.multiple_of(g * COLS, COLS), COLS)]
        return pltpu.make_async_copy(src, local_w.at[i, g], sem_l.at[i, g])

    late_copies = [
        pltpu.make_async_copy(src, weights.at[i], sem_w.at[i])
        for i, src in enumerate((wout_hbm, cq, ck, cv))
    ]

    def out_copy(g):
        dst = att.at[:, pl.ds(pl.multiple_of(g * COLS, COLS), COLS)]
        return pltpu.make_async_copy(att_out.at[g], dst, sem_o.at[g])

    @pl.when(step == 0)
    def _():
        embed_copy.start()
        for g in range(steps):
            for i in range(3):
                local_copy(i, g).start()
        for copy in late_copies:
            copy.start()
        fill_one_hot(hot, 0, low[...].reshape(1, HALF_WIN))
        for c in range(0, rows, HALF_WIN):
            part = own[c : c + HALF_WIN].reshape(1, HALF_WIN)
            fill_one_hot(hot, HALF_WIN + c, part)
        fill_one_hot(hot, HALF_WIN + rows, high[...].reshape(1, HALF_WIN))
        near = SUB + 2 * HALF_WIN
        ahead = lax.broadcasted_iota(jnp.int32, (near, SUB), 0) - lax.broadcasted_iota(
            jnp.int32, (near, SUB), 1
        )
        band = jnp.where((ahead >= 0) & (ahead <= 2 * HALF_WIN), 1.0, 0.0).astype(BF16)
        for t in range(rows // SUB):
            count = dot(hot[:, t * SUB : t * SUB + near], band)
            for s in chunks(ROWS):
                c = count[s]
                logs[s, t * SUB : (t + 1) * SUB] = jnp.where(
                    c > 0.0, jnp.log(jnp.maximum(c, 1.0)) * math.log2(math.e), -1e30
                )
        row = lax.broadcasted_iota(jnp.int32, (16, rows), 0)
        col = lax.broadcasted_iota(jnp.int32, (16, rows), 1)
        member = jnp.where(col // POOL == row, 1.0 / POOL, 0.0).astype(BF16)
        share = dot_nt(member, hot[:, HALF_WIN : HALF_WIN + rows])
        embed_copy.wait()
        mask_row = mask_embed[...].reshape(1, D)
        gain_row = gain[...].reshape(1, D)
        pooled_in[...] = dot(share[:, 0:VOCAB].astype(BF16), embed[...]) + share[
            :, VOCAB : VOCAB + 1
        ] * mask_row.astype(F32)
        for c in range(0, VOCAB, 32):
            normed[c : c + 32, :] = normalize(embed[c : c + 32], gain_row)
        keep = lax.broadcasted_iota(jnp.int32, (16, D), 0) == 0
        row = jnp.broadcast_to(normalize(mask_row, gain_row).astype(F32), (16, D))
        normed[VOCAB:ROWS, :] = jnp.where(keep, row, 0.0).astype(BF16)

    for i in range(3):
        local_copy(i, step).wait()
    q = rounded(dot(normed[...], local_w[0, step]))
    qt = q[0:VOCAB].T.astype(BF16)
    qm = jnp.broadcast_to(q[VOCAB : VOCAB + 1], (128, COLS)).T
    k_all = dot(normed[...], local_w[1, step])
    for c in chunks(ROWS):
        k = rounded(k_all[c]) * (math.log2(math.e) * WIDTH**-0.5)
        k_a = k.astype(BF16)
        k_b = (k - k_a.astype(F32)).astype(BF16)
        for h in range(GROUP):
            s = slice(h * WIDTH, (h + 1) * WIDTH)
            k2[h, c] = jnp.concatenate([k_a[:, s], k_b[:, s]], axis=1)
    v = rounded(dot(normed[...], local_w[2, step]))
    v_t = v[0:VOCAB].T
    v_m = jnp.broadcast_to(v[VOCAB : VOCAB + 1], (128, COLS)).T
    ones = jnp.where(lax.broadcasted_iota(jnp.int32, (16, VOCAB), 0) == 0, 1.0, 0.0)
    vm = []
    for h in range(GROUP):
        s = slice(h * WIDTH, (h + 1) * WIDTH)
        vt[h] = jnp.concatenate([v_t[s], ones], axis=0).astype(BF16)
        vm.append(jnp.concatenate([v_m[s], ones[:, 0:128]], axis=0))

    queries = []
    for t in range(rows // TILE):
        own_cols = slice(HALF_WIN + t * TILE, HALF_WIN + (t + 1) * TILE)
        masked = hot[VOCAB:ROWS, own_cols].astype(F32)[0:1]
        x = dot(qt, hot[0:VOCAB, own_cols])
        x = x + jnp.concatenate([qm] * (TILE // 128), axis=1) * masked
        queries.append(x.astype(BF16))

    units = [(t, h) for t in range(rows // TILE) for h in range(GROUP)]

    def score(u):
        t, h = units[u]
        q_h = queries[t][h * WIDTH : (h + 1) * WIDTH]
        s = dot(k2[h], jnp.concatenate([q_h, q_h], axis=0))
        top = None
        for c in chunks(ROWS):
            part = s[c] + logs[c, t * TILE : (t + 1) * TILE]
            scores[u % 2, c] = part
            peak = jnp.max(part.reshape((c.stop - c.start) // 8, 8, TILE), axis=0)
            top = peak if top is None else jnp.maximum(top, peak)
        return jnp.max(top, axis=0, keepdims=True)

    def mix(u, top):
        h = units[u][1]
        for c in chunks(ROWS):
            probs[u % 2, c] = jnp.exp2((scores[u % 2, c] - top).astype(BF16))
        mixed = dot(vt[h], probs[u % 2, 0:VOCAB])
        last = probs[u % 2, VOCAB:ROWS].astype(F32)[0:1]
        mixed = mixed + jnp.concatenate([vm[h]] * (TILE // 128), axis=1) * last
        return mixed[0:WIDTH] * (1.0 / mixed[WIDTH : WIDTH + 1])

    top = score(0)
    held = None
    for u, (t, h) in enumerate(units):
        later = score(u + 1) if u + 1 < len(units) else None
        mixed = mix(u, top)
        top = later
        if h % 2 == 0:
            held = mixed
            continue
        out = jnp.concatenate([held, mixed], axis=0).T
        cols = slice((h - 1) * WIDTH, (h + 1) * WIDTH)
        att_out[step, t * TILE : (t + 1) * TILE, cols] = out.astype(BF16)
        each = TILE // POOL
        mean = jnp.sum(out.reshape(each, POOL, 128), axis=1) * (1.0 / POOL)
        matt[step, t * each : (t + 1) * each, cols] = mean
    out_copy(step).start()

    @pl.when(step == steps - 1)
    def _():
        for copy in late_copies:
            copy.wait()
        mean = jnp.concatenate([matt[g] for g in range(steps)], axis=1)
        head = mean.astype(BF16)
        tail = (mean - head.astype(F32)).astype(BF16)
        lifted = dot(jnp.concatenate([head, tail], axis=0), weights[0])
        pooled = (pooled_in[...] + lifted[0:16] + lifted[16:32]).astype(BF16)
        coarse = normalize(pooled, cgain[...].reshape(1, D))
        q = rounded(dot(coarse, weights[1]))
        k = rounded(dot(coarse, weights[2]))
        v = rounded(dot(coarse, weights[3]))
        for h in range(HEADS):
            s = slice(h * WIDTH, (h + 1) * WIDTH)
            kv = jnp.concatenate([k[:, s], v[:, s]], axis=1)
            qq = jnp.concatenate([q[0:8, s], q[8:16, s]], axis=1)
            payload[h] = jnp.concatenate([kv, qq], axis=0).astype(BF16)
        for g in range(steps):
            out_copy(g).wait()


def local_attention(low, own, high, mask_embed, gain, cgain, *arrays):
    steps = HEADS // GROUP
    rows = own.shape[0]
    whole = lambda shape: pl.BlockSpec(shape, lambda g: (0,) * len(shape))
    hbm = pl.BlockSpec(memory_space=pl.ANY)
    small = (low, own, high, mask_embed, gain, cgain)
    return pl.pallas_call(
        local_kernel,
        grid=(steps,),
        in_specs=[whole(x.shape) for x in small] + [hbm] * len(arrays),
        out_specs=[hbm, whole((HEADS, 24, 128))],
        out_shape=[
            jax.ShapeDtypeStruct((rows, D), BF16),
            jax.ShapeDtypeStruct((HEADS, 24, 128), BF16),
        ],
        scratch_shapes=[
            pltpu.VMEM((ROWS, rows + 2 * HALF_WIN), BF16),
            pltpu.VMEM((ROWS, rows), F32),
            pltpu.VMEM((2, ROWS, TILE), F32),
            pltpu.VMEM((2, ROWS, TILE), BF16),
            pltpu.VMEM((16, D), F32),
            pltpu.VMEM((steps, rows // POOL, COLS), F32),
            pltpu.VMEM((VOCAB, D), BF16),
            pltpu.VMEM((3, steps, D, COLS), BF16),
            pltpu.VMEM((4, D, D), BF16),
            pltpu.VMEM((ROWS, D), BF16),
            pltpu.VMEM((GROUP, ROWS, 2 * WIDTH), BF16),
            pltpu.VMEM((GROUP, VROWS, VOCAB), BF16),
            pltpu.VMEM((steps, rows, COLS), BF16),
            pltpu.SemaphoreType.DMA(()),
            pltpu.SemaphoreType.DMA((3, steps)),
            pltpu.SemaphoreType.DMA((4,)),
            pltpu.SemaphoreType.DMA((steps,)),
        ],
        compiler_params=pltpu.CompilerParams(vmem_limit_bytes=60 * MIB),
        cost_estimate=pl.CostEstimate(
            flops=16 * rows * ROWS * D, bytes_accessed=20 * MIB, transcendentals=rows * ROWS * HEADS
        ),
        name="local",
    )(*small, *arrays)


def mid_kernel(ids, att, embed, mask_embed, wout, mid):
    hot = one_hot(ids[...].reshape(1, SUB))
    total = dot(att[...], wout[...]) + dot_tn(hot[0:VOCAB], embed[...])
    row = jnp.broadcast_to(mask_embed[...].reshape(1, D), (16, D))
    total = total + dot_tn(hot[VOCAB:ROWS], row)
    mid[...] = total.astype(BF16)


def make_mid(ids, att, embed, mask_embed, wout):
    rows = att.shape[0]
    whole = lambda shape: pl.BlockSpec(shape, lambda g: (0,) * len(shape))
    return pl.pallas_call(
        mid_kernel,
        grid=(rows // SUB,),
        in_specs=[
            pl.BlockSpec((SUB,), lambda g: (g,)),
            pl.BlockSpec((SUB, D), lambda g: (g, 0)),
            whole((VOCAB, D)),
            whole((D,)),
            whole((D, D)),
        ],
        out_specs=pl.BlockSpec((SUB, D), lambda g: (g, 0)),
        out_shape=jax.ShapeDtypeStruct((rows, D), BF16),
        compiler_params=pltpu.CompilerParams(vmem_limit_bytes=60 * MIB),
        cost_estimate=pl.CostEstimate(
            flops=2 * rows * (ROWS + D) * D, bytes_accessed=8 * MIB, transcendentals=0
        ),
        name="mid",
    )(ids, att, embed, mask_embed, wout)


def coarse_kernel(q, kv, out):
    x = q[...].astype(F32).reshape(q.shape[0] * 8, 128) * WIDTH**-0.5
    low = lax.broadcasted_iota(jnp.int32, x.shape, 1) < WIDTH
    both = jnp.concatenate(
        [jnp.where(low, x, 0.0), jnp.where(low, pltpu.roll(x, WIDTH, 1), 0.0)], axis=0
    ).astype(BF16)
    scores = dot_nt(both, kv[...])
    probs = jnp.exp(scores - jnp.max(scores, axis=1, keepdims=True))
    total = jnp.sum(probs, axis=1, keepdims=True)
    mixed = dot(probs.astype(BF16), kv[...]) * (1.0 / total)
    half = x.shape[0]
    packed = jnp.where(low, pltpu.roll(mixed[0:half], WIDTH, 1), mixed[half:])
    out[...] = packed.reshape(out.shape).astype(BF16)


def coarse_attention(q, kv):
    vmem = pl.BlockSpec(memory_space=pltpu.VMEM)
    return pl.pallas_call(
        coarse_kernel,
        in_specs=[vmem, vmem],
        out_shape=jax.ShapeDtypeStruct(q.shape, BF16),
        compiler_params=pltpu.CompilerParams(vmem_limit_bytes=32 * MIB),
        cost_estimate=pl.CostEstimate(
            flops=8 * 10**9, bytes_accessed=16 * MIB, transcendentals=1 << 19
        ),
        name="coarse",
    )(q, kv)


def final_kernel(back, wout, mid, out, lifted):
    step = pl.program_id(0)

    @pl.when(step == 0)
    def _():
        low = lax.broadcasted_iota(jnp.int32, (8, 128), 1) < WIDTH
        top, bottom = [], []
        for pair in range(HEADS // 2):
            a = back[2 * pair].astype(F32)
            b = back[2 * pair + 1].astype(F32)
            top.append(jnp.where(low, a, pltpu.roll(b, WIDTH, 1)))
            bottom.append(jnp.where(low, pltpu.roll(a, WIDTH, 1), b))
        rows = [jnp.concatenate(top, axis=1), jnp.concatenate(bottom, axis=1)]
        lifted[...] = dot(jnp.concatenate(rows, axis=0).astype(BF16), wout[...])

    each = mid.shape[0] // POOL
    for r in range(each):
        s = slice(r * POOL, (r + 1) * POOL)
        add = lifted[pl.ds(step * each + r, 1), :]
        out[s, :] = (mid[s, :].astype(F32) + add).astype(BF16)


def finish(back, wout, mid):
    rows = mid.shape[0]
    whole = lambda shape: pl.BlockSpec(shape, lambda g: (0,) * len(shape))
    return pl.pallas_call(
        final_kernel,
        grid=(rows // SUB,),
        in_specs=[
            whole(back.shape),
            whole((D, D)),
            pl.BlockSpec((SUB, D), lambda g: (g, 0)),
        ],
        out_specs=pl.BlockSpec((SUB, D), lambda g: (g, 0)),
        out_shape=jax.ShapeDtypeStruct((rows, D), BF16),
        scratch_shapes=[pltpu.VMEM((16, D), F32)],
        compiler_params=pltpu.CompilerParams(vmem_limit_bytes=20 * MIB),
        name="finish",
    )(back, wout, mid)


def body(
    token_ids,
    bar_mask,
    embed,
    mask_embed,
    local_gain,
    local_query,
    local_key,
    local_value,
    local_out,
    coarse_gain,
    coarse_query,
    coarse_key,
    coarse_value,
    coarse_out,
):
    rows = token_ids.shape[0]
    own = jnp.where(bar_mask == 1, VOCAB + 1, token_ids + 1)
    count = lax.axis_size(ALL)
    here = lax.axis_index(ALL)
    forward = [(i, (i + 1) % count) for i in range(count)]
    backward = [(b, a) for a, b in forward]
    low = lax.ppermute(jnp.where(here == count - 1, 0, own[rows - HALF_WIN :]), ALL, forward)
    high = lax.ppermute(jnp.where(here == 0, 0, own[:HALF_WIN]), ALL, backward)
    att, payload = local_attention(
        low, own, high, mask_embed, local_gain, coarse_gain, embed,
        local_query, local_key, local_value, local_out, coarse_query, coarse_key, coarse_value,
    )
    got = lax.all_to_all(payload, PLANE, split_axis=0, concat_axis=0, tiled=True)
    q = got[:, 16:24]
    kv = got[:, 0:16].reshape(1, HEADS * 16, 128)
    peers = lax.axis_size(RING)
    kv = jnp.broadcast_to(kv, (peers,) + kv.shape[1:])
    kv = lax.all_to_all(kv, RING, split_axis=0, concat_axis=0, tiled=True)
    mid = make_mid(own, att, embed, mask_embed, local_out)
    kv, mid = lax.optimization_barrier((kv, mid))
    mixed = coarse_attention(q, kv.reshape(peers * HEADS * 16, 128))
    back = lax.all_to_all(mixed, PLANE, split_axis=0, concat_axis=0, tiled=True)
    return finish(back, coarse_out, mid)


def solution(mesh):
    fine = Mesh(mesh.devices.reshape((2,) * len(ALL)), ALL)
    placed = (P(ALL),) * 2 + (P(),) * 12
    return jax.shard_map(
        body, mesh=fine, in_specs=placed, out_specs=P(ALL, None), check_vma=False
    )
```

```python
import functools
import math

import jax
import jax.numpy as jnp
from jax import lax
from jax.experimental import pallas as pl
from jax.experimental.pallas import tpu as pltpu
from jax.sharding import Mesh
from jax.sharding import PartitionSpec as P

D = 1024
HEADS = 16
WIDTH = 64
VOCAB = 512
ROWS = VOCAB + 16
HALF_WIN = 512
POOL = 64
TILE = 512
SUB = 256
CHUNK = 48
GROUP = 4
COLS = GROUP * WIDTH
VROWS = WIDTH + 16
MIB = 1 << 20
ALL = ("x_hi", "x_lo", "y_hi", "z_hi", "z_lo", "y_lo", "core")
RING = ("z_hi", "z_lo", "core")
PLANE = ("x_hi", "x_lo", "y_hi", "y_lo")
F32 = jnp.float32
BF16 = jnp.bfloat16


def dot(a, b):
    return jnp.dot(a, b, preferred_element_type=F32)


def dot_nt(a, b):
    return lax.dot_general(a, b, (((1,), (1,)), ((), ())), preferred_element_type=F32)


def dot_tn(a, b):
    return lax.dot_general(a, b, (((0,), (0,)), ((), ())), preferred_element_type=F32)


def normalize(rows, gain):
    wide = rows.astype(F32)
    scaled = wide * lax.rsqrt(jnp.mean(wide * wide, axis=-1, keepdims=True) + 1e-05)
    return (scaled * gain.astype(F32)).astype(BF16)


def rounded(x):
    return x.astype(BF16).astype(F32)


def chunks(rows):
    return [slice(c, min(c + CHUNK, rows)) for c in range(0, rows, CHUNK)]


def fill_one_hot(out, first, ids):
    count = ids.shape[1]
    for s in chunks(ROWS):
        event = lax.broadcasted_iota(jnp.int32, (s.stop - s.start, count), 0) + (s.start + 1)
        out[s, first : first + count] = jnp.where(event == ids, 1.0, 0.0).astype(BF16)


def local_kernel(
    low, own, high, mask_embed, gain, cgain, embed_hbm, lq, lk, lv, wout_hbm, cq, ck, cv,
    att, payload,
    hot, logs, scores, probs, pooled_in, matt, embed, local_w, weights, normed, k2, vt, att_out,
    sem_e, sem_l, sem_w, sem_o,
):
    step = pl.program_id(0)
    rows = att.shape[0]
    steps = HEADS // GROUP
    embed_copy = pltpu.make_async_copy(embed_hbm, embed, sem_e)

    def local_copy(i, g):
        src = (lq, lk, lv)[i].at[:, pl.ds(pl.multiple_of(g * COLS, COLS), COLS)]
        return pltpu.make_async_copy(src, local_w.at[i, g], sem_l.at[i, g])

    late_copies = [
        pltpu.make_async_copy(src, weights.at[i], sem_w.at[i])
        for i, src in enumerate((wout_hbm, cq, ck, cv))
    ]

    def out_copy(g):
        dst = att.at[:, pl.ds(pl.multiple_of(g * COLS, COLS), COLS)]
        return pltpu.make_async_copy(att_out.at[g], dst, sem_o.at[g])

    @pl.when(step == 0)
    def _():
        embed_copy.start()
        for g in range(steps):
            for i in range(3):
                local_copy(i, g).start()
        for copy in late_copies:
            copy.start()
        fill_one_hot(hot, 0, low[...].reshape(1, HALF_WIN))
        for c in range(0, rows, HALF_WIN):
            part = own[c : c + HALF_WIN].reshape(1, HALF_WIN)
            fill_one_hot(hot, HALF_WIN + c, part)
        fill_one_hot(hot, HALF_WIN + rows, high[...].reshape(1, HALF_WIN))
        j = lax.broadcasted_iota(jnp.int32, (SUB, SUB), 0)
        i = lax.broadcasted_iota(jnp.int32, (SUB, SUB), 1)
        first = jnp.where(j >= i, 1.0, 0.0).astype(BF16)
        last = jnp.where(j <= i, 1.0, 0.0).astype(BF16)
        every = jnp.ones((SUB, SUB), BF16)
        span = 2 * HALF_WIN // SUB
        for t in range(rows // SUB):
            block = lambda b: hot[:, (t + b) * SUB : (t + b + 1) * SUB]
            inner = block(1)
            for b in range(2, span):
                inner = inner + block(b)
            count = dot(block(0), first) + dot(inner, every) + dot(block(span), last)
            for s in chunks(ROWS):
                c = count[s]
                logs[s, t * SUB : (t + 1) * SUB] = jnp.where(
                    c > 0.0, jnp.log(jnp.maximum(c, 1.0)) * math.log2(math.e), -1e30
                )
        row = lax.broadcasted_iota(jnp.int32, (16, rows), 0)
        col = lax.broadcasted_iota(jnp.int32, (16, rows), 1)
        member = jnp.where(col // POOL == row, 1.0 / POOL, 0.0).astype(BF16)
        share = dot_nt(member, hot[:, HALF_WIN : HALF_WIN + rows])
        embed_copy.wait()
        mask_row = mask_embed[...].reshape(1, D)
        gain_row = gain[...].reshape(1, D)
        pooled_in[...] = dot(share[:, 0:VOCAB].astype(BF16), embed[...]) + share[
            :, VOCAB : VOCAB + 1
        ] * mask_row.astype(F32)
        for c in range(0, VOCAB, 32):
            normed[c : c + 32, :] = normalize(embed[c : c + 32], gain_row)
        keep = lax.broadcasted_iota(jnp.int32, (16, D), 0) == 0
        row = jnp.broadcast_to(normalize(mask_row, gain_row).astype(F32), (16, D))
        normed[VOCAB:ROWS, :] = jnp.where(keep, row, 0.0).astype(BF16)

    for i in range(3):
        local_copy(i, step).wait()
    q = rounded(dot(normed[...], local_w[0, step]))
    qt = q[0:VOCAB].T.astype(BF16)
    qm = jnp.broadcast_to(q[VOCAB : VOCAB + 1], (128, COLS)).T
    k_all = dot(normed[...], local_w[1, step])
    for c in chunks(ROWS):
        k = rounded(k_all[c]) * (math.log2(math.e) * WIDTH**-0.5)
        k_a = k.astype(BF16)
        k_b = (k - k_a.astype(F32)).astype(BF16)
        for h in range(GROUP):
            s = slice(h * WIDTH, (h + 1) * WIDTH)
            k2[h, c] = jnp.concatenate([k_a[:, s], k_b[:, s]], axis=1)
    v = rounded(dot(normed[...], local_w[2, step]))
    v_t = v[0:VOCAB].T
    v_m = jnp.broadcast_to(v[VOCAB : VOCAB + 1], (128, COLS)).T
    ones = jnp.where(lax.broadcasted_iota(jnp.int32, (16, VOCAB), 0) == 0, 1.0, 0.0)
    vm = []
    for h in range(GROUP):
        s = slice(h * WIDTH, (h + 1) * WIDTH)
        vt[h] = jnp.concatenate([v_t[s], ones], axis=0).astype(BF16)
        vm.append(jnp.concatenate([v_m[s], ones[:, 0:128]], axis=0))

    queries = []
    for t in range(rows // TILE):
        own_cols = slice(HALF_WIN + t * TILE, HALF_WIN + (t + 1) * TILE)
        masked = hot[VOCAB:ROWS, own_cols].astype(F32)[0:1]
        x = dot(qt, hot[0:VOCAB, own_cols])
        x = x + jnp.concatenate([qm] * (TILE // 128), axis=1) * masked
        queries.append(x.astype(BF16))

    units = [(t, h) for t in range(rows // TILE) for h in range(GROUP)]

    def score(u):
        t, h = units[u]
        q_h = queries[t][h * WIDTH : (h + 1) * WIDTH]
        s = dot(k2[h], jnp.concatenate([q_h, q_h], axis=0))
        top = None
        for c in chunks(ROWS):
            part = s[c] + logs[c, t * TILE : (t + 1) * TILE]
            scores[u % 2, c] = part
            peak = jnp.max(part.reshape((c.stop - c.start) // 8, 8, TILE), axis=0)
            top = peak if top is None else jnp.maximum(top, peak)
        return jnp.max(top, axis=0, keepdims=True)

    def mix(u, top):
        h = units[u][1]
        for c in chunks(ROWS):
            probs[u % 2, c] = jnp.exp2((scores[u % 2, c] - top).astype(BF16))
        mixed = dot(vt[h], probs[u % 2, 0:VOCAB])
        last = probs[u % 2, VOCAB:ROWS].astype(F32)[0:1]
        mixed = mixed + jnp.concatenate([vm[h]] * (TILE // 128), axis=1) * last
        return mixed[0:WIDTH] * (1.0 / mixed[WIDTH : WIDTH + 1])

    top = score(0)
    held = None
    for u, (t, h) in enumerate(units):
        later = score(u + 1) if u + 1 < len(units) else None
        mixed = mix(u, top)
        top = later
        if h % 2 == 0:
            held = mixed
            continue
        out = jnp.concatenate([held, mixed], axis=0).T
        cols = slice((h - 1) * WIDTH, (h + 1) * WIDTH)
        att_out[step, t * TILE : (t + 1) * TILE, cols] = out.astype(BF16)
        each = TILE // POOL
        mean = jnp.sum(out.reshape(each, POOL, 128), axis=1) * (1.0 / POOL)
        matt[step, t * each : (t + 1) * each, cols] = mean
    out_copy(step).start()

    @pl.when(step == steps - 1)
    def _():
        for copy in late_copies:
            copy.wait()
        mean = jnp.concatenate([matt[g] for g in range(steps)], axis=1)
        head = mean.astype(BF16)
        tail = (mean - head.astype(F32)).astype(BF16)
        lifted = dot(jnp.concatenate([head, tail], axis=0), weights[0])
        pooled = (pooled_in[...] + lifted[0:16] + lifted[16:32]).astype(BF16)
        coarse = normalize(pooled, cgain[...].reshape(1, D))
        q = rounded(dot(coarse, weights[1]))
        k = rounded(dot(coarse, weights[2]))
        v = rounded(dot(coarse, weights[3]))
        for h in range(HEADS):
            s = slice(h * WIDTH, (h + 1) * WIDTH)
            kv = jnp.concatenate([k[:, s], v[:, s]], axis=1)
            qq = jnp.concatenate([q[0:8, s], q[8:16, s]], axis=1)
            payload[h] = jnp.concatenate([kv, qq], axis=0).astype(BF16)
        for g in range(steps):
            out_copy(g).wait()


def local_attention(low, own, high, mask_embed, gain, cgain, *arrays):
    steps = HEADS // GROUP
    rows = own.shape[0]
    whole = lambda shape: pl.BlockSpec(shape, lambda g: (0,) * len(shape))
    hbm = pl.BlockSpec(memory_space=pl.ANY)
    small = (low, own, high, mask_embed, gain, cgain)
    return pl.pallas_call(
        local_kernel,
        grid=(steps,),
        in_specs=[whole(x.shape) for x in small] + [hbm] * len(arrays),
        out_specs=[hbm, whole((HEADS, 24, 128))],
        out_shape=[
            jax.ShapeDtypeStruct((rows, D), BF16),
            jax.ShapeDtypeStruct((HEADS, 24, 128), BF16),
        ],
        scratch_shapes=[
            pltpu.VMEM((ROWS, rows + 2 * HALF_WIN), BF16),
            pltpu.VMEM((ROWS, rows), F32),
            pltpu.VMEM((2, ROWS, TILE), F32),
            pltpu.VMEM((2, ROWS, TILE), BF16),
            pltpu.VMEM((16, D), F32),
            pltpu.VMEM((steps, rows // POOL, COLS), F32),
            pltpu.VMEM((VOCAB, D), BF16),
            pltpu.VMEM((3, steps, D, COLS), BF16),
            pltpu.VMEM((4, D, D), BF16),
            pltpu.VMEM((ROWS, D), BF16),
            pltpu.VMEM((GROUP, ROWS, 2 * WIDTH), BF16),
            pltpu.VMEM((GROUP, VROWS, VOCAB), BF16),
            pltpu.VMEM((steps, rows, COLS), BF16),
            pltpu.SemaphoreType.DMA(()),
            pltpu.SemaphoreType.DMA((3, steps)),
            pltpu.SemaphoreType.DMA((4,)),
            pltpu.SemaphoreType.DMA((steps,)),
        ],
        compiler_params=pltpu.CompilerParams(vmem_limit_bytes=60 * MIB),
        cost_estimate=pl.CostEstimate(
            flops=16 * rows * ROWS * D, bytes_accessed=20 * MIB, transcendentals=rows * ROWS * HEADS
        ),
        name="local",
    )(*small, *arrays)


def mid_kernel(
    ids, mask_embed, embed_hbm, wout_hbm, att_hbm, mid_hbm, total, embed, wout, att, out, sems
):
    rows = att.shape[0]
    tiles = [slice(c, c + SUB) for c in range(0, rows, SUB)]
    embed_copy = pltpu.make_async_copy(embed_hbm, embed, sems.at[0])
    wout_copy = pltpu.make_async_copy(wout_hbm, wout, sems.at[1])
    att_copies = [
        pltpu.make_async_copy(att_hbm.at[s], att.at[s], sems.at[2 + t])
        for t, s in enumerate(tiles)
    ]
    out_copies = [
        pltpu.make_async_copy(out.at[s], mid_hbm.at[s], sems.at[2 + len(tiles) + t])
        for t, s in enumerate(tiles)
    ]
    for copy in [embed_copy, wout_copy] + att_copies:
        copy.start()
    own = jnp.broadcast_to(ids[...].reshape(1, rows).astype(F32), (128, rows)).T
    lane = lax.broadcasted_iota(jnp.int32, (SUB, 128), 1).astype(F32)
    mask_row = mask_embed[...].reshape(1, D).astype(F32)
    embed_copy.wait()
    for s in tiles:
        hot = [jnp.where(own[s] == lane + (b + 1), 1.0, 0.0) for b in range(0, VOCAB, 128)]
        hot = jnp.concatenate(hot, axis=1).astype(BF16)
        masked = jnp.where(own[s] == VOCAB + 1.0, 1.0, 0.0)
        masked = jnp.concatenate([masked] * (D // 128), axis=1)
        total[s, :] = dot(hot, embed[...]) + masked * mask_row
    wout_copy.wait()
    for t, s in enumerate(tiles):
        att_copies[t].wait()
        out[s, :] = (total[s, :] + dot(att[s, :], wout[...])).astype(BF16)
        out_copies[t].start()
    for copy in out_copies:
        copy.wait()


def make_mid(ids, att, embed, mask_embed, wout):
    rows = att.shape[0]
    vmem = pl.BlockSpec(memory_space=pltpu.VMEM)
    hbm = pl.BlockSpec(memory_space=pl.ANY)
    return pl.pallas_call(
        mid_kernel,
        in_specs=[vmem, vmem, hbm, hbm, hbm],
        out_specs=hbm,
        out_shape=jax.ShapeDtypeStruct((rows, D), BF16),
        scratch_shapes=[
            pltpu.VMEM((rows, D), F32),
            pltpu.VMEM((VOCAB, D), BF16),
            pltpu.VMEM((D, D), BF16),
            pltpu.VMEM((rows, D), BF16),
            pltpu.VMEM((rows, D), BF16),
            pltpu.SemaphoreType.DMA((2 + 2 * (rows // SUB),)),
        ],
        compiler_params=pltpu.CompilerParams(vmem_limit_bytes=60 * MIB),
        cost_estimate=pl.CostEstimate(
            flops=2 * rows * (ROWS + D) * D, bytes_accessed=8 * MIB, transcendentals=0
        ),
        name="mid",
    )(ids, mask_embed, embed, wout, att)


def coarse_kernel(q, kv, out):
    x = q[...].astype(F32).reshape(q.shape[0] * 8, 128) * WIDTH**-0.5
    low = lax.broadcasted_iota(jnp.int32, x.shape, 1) < WIDTH
    both = jnp.concatenate(
        [jnp.where(low, x, 0.0), jnp.where(low, pltpu.roll(x, WIDTH, 1), 0.0)], axis=0
    ).astype(BF16)
    scores = dot_nt(both, kv[...])
    probs = jnp.exp(scores - jnp.max(scores, axis=1, keepdims=True))
    total = jnp.sum(probs, axis=1, keepdims=True)
    mixed = dot(probs.astype(BF16), kv[...]) * (1.0 / total)
    half = x.shape[0]
    packed = jnp.where(low, pltpu.roll(mixed[0:half], WIDTH, 1), mixed[half:])
    out[...] = packed.reshape(out.shape).astype(BF16)


def coarse_attention(q, kv):
    vmem = pl.BlockSpec(memory_space=pltpu.VMEM)
    return pl.pallas_call(
        coarse_kernel,
        in_specs=[vmem, vmem],
        out_shape=jax.ShapeDtypeStruct(q.shape, BF16),
        compiler_params=pltpu.CompilerParams(vmem_limit_bytes=32 * MIB),
        cost_estimate=pl.CostEstimate(
            flops=8 * 10**9, bytes_accessed=16 * MIB, transcendentals=1 << 19
        ),
        name="coarse",
    )(q, kv)


def final_kernel(back, wout, mid, out, lifted):
    step = pl.program_id(0)

    @pl.when(step == 0)
    def _():
        low = lax.broadcasted_iota(jnp.int32, (8, 128), 1) < WIDTH
        top, bottom = [], []
        for pair in range(HEADS // 2):
            a = back[2 * pair].astype(F32)
            b = back[2 * pair + 1].astype(F32)
            top.append(jnp.where(low, a, pltpu.roll(b, WIDTH, 1)))
            bottom.append(jnp.where(low, pltpu.roll(a, WIDTH, 1), b))
        rows = [jnp.concatenate(top, axis=1), jnp.concatenate(bottom, axis=1)]
        lifted[...] = dot(jnp.concatenate(rows, axis=0).astype(BF16), wout[...])

    each = mid.shape[0] // POOL
    for r in range(each):
        s = slice(r * POOL, (r + 1) * POOL)
        add = lifted[pl.ds(step * each + r, 1), :]
        out[s, :] = (mid[s, :].astype(F32) + add).astype(BF16)


def finish(back, wout, mid):
    rows = mid.shape[0]
    whole = lambda shape: pl.BlockSpec(shape, lambda g: (0,) * len(shape))
    return pl.pallas_call(
        final_kernel,
        grid=(rows // SUB,),
        in_specs=[
            whole(back.shape),
            whole((D, D)),
            pl.BlockSpec((SUB, D), lambda g: (g, 0)),
        ],
        out_specs=pl.BlockSpec((SUB, D), lambda g: (g, 0)),
        out_shape=jax.ShapeDtypeStruct((rows, D), BF16),
        scratch_shapes=[pltpu.VMEM((16, D), F32)],
        compiler_params=pltpu.CompilerParams(vmem_limit_bytes=20 * MIB),
        name="finish",
    )(back, wout, mid)


def body(
    token_ids,
    bar_mask,
    embed,
    mask_embed,
    local_gain,
    local_query,
    local_key,
    local_value,
    local_out,
    coarse_gain,
    coarse_query,
    coarse_key,
    coarse_value,
    coarse_out,
):
    rows = token_ids.shape[0]
    own = jnp.where(bar_mask == 1, VOCAB + 1, token_ids + 1)
    count = lax.axis_size(ALL)
    here = lax.axis_index(ALL)
    forward = [(i, (i + 1) % count) for i in range(count)]
    backward = [(b, a) for a, b in forward]
    low = lax.ppermute(jnp.where(here == count - 1, 0, own[rows - HALF_WIN :]), ALL, forward)
    high = lax.ppermute(jnp.where(here == 0, 0, own[:HALF_WIN]), ALL, backward)
    att, payload = local_attention(
        low, own, high, mask_embed, local_gain, coarse_gain, embed,
        local_query, local_key, local_value, local_out, coarse_query, coarse_key, coarse_value,
    )
    got = lax.all_to_all(payload, PLANE, split_axis=0, concat_axis=0, tiled=True)
    q = got[:, 16:24]
    kv = got[:, 0:16].reshape(1, HEADS * 16, 128)
    peers = lax.axis_size(RING)
    kv = jnp.broadcast_to(kv, (peers,) + kv.shape[1:])
    kv = lax.all_to_all(kv, RING, split_axis=0, concat_axis=0, tiled=True)
    mid = make_mid(own, att, embed, mask_embed, local_out)
    kv, mid = lax.optimization_barrier((kv, mid))
    mixed = coarse_attention(q, kv.reshape(peers * HEADS * 16, 128))
    back = lax.all_to_all(mixed, PLANE, split_axis=0, concat_axis=0, tiled=True)
    return finish(back, coarse_out, mid)


def solution(mesh):
    fine = Mesh(mesh.devices.reshape((2,) * len(ALL)), ALL)
    placed = (P(ALL),) * 2 + (P(),) * 12
    return jax.shard_map(
        body, mesh=fine, in_specs=placed, out_specs=P(ALL, None), check_vma=False
    )
```
